256 devices in a mesh: dp: 4 (over y), mp: 64 (over x, z, core).
Axes of the slice: x: 4, y: 4, z: 8, core: 2. Of those that a mesh axis runs over, the one named last changes fastest.
Arguments:
- gate: bfloat16 [2048, 14336], P('dp', 'mp'), may hold values from -6 to 6
- upward: bfloat16 [2048, 14336], P('dp', 'mp'), may hold values from -6 to 6
- cotangent: bfloat16 [2048, 8192], P('dp', 'mp'), may hold values from -4 to 4
- down_weight: bfloat16 [14336, 8192], P('mp'), may hold values from -0.046875 to 0.046875
- error_buffer: bfloat16 [4, 14336, 8192], P('dp', 'mp'), may hold values from -24 to 24
- start_q: float32 [14336, 32], P('mp'), may hold values from -0.046875 to 0.046875
Outputs:
- d_gate: bfloat16 [2048, 14336], P('dp', 'mp')
- d_up: bfloat16 [2048, 14336], P('dp', 'mp')
- new_error: bfloat16 [4, 14336, 8192], P('dp', 'mp')
- next_q: float32 [14336, 32], P('mp')
The draws below stay inside these ranges and needn't reach their ends.
All inputs are finite; a program needn't handle non-finite values.
Results may differ from the reference program's by a relative error of at most 0.0065.
Values may be sent and summed in bfloat16 or wider, within the bound.
No kernel may reach another device: no remote copies, remote signals or barrier semaphores. Data moves between devices by JAX's collectives and lax.ppermute only.
A program may use at most 128 MiB of HBM per device.

```python
import jax
import jax.numpy as jnp
from jax import lax

D = 8192
FF = 14336
RANK = 32
TOK = 512
TOKENS = 2048
N_DP = 4


def block_scale(key, dims, pieces, least, largest):
    loudness, own = 1.0, jax.random.fold_in(key, 6)
    for axis_at, blocks in pieces:
        steps = jnp.exp(jax.random.uniform(jax.random.fold_in(own, axis_at), (blocks,), jnp.float32, least / len(pieces), largest / len(pieces)))
        loudness = loudness * jnp.repeat(steps, dims[axis_at] // blocks).reshape([-1 if axis == axis_at else 1 for axis in range(len(dims))])
    return loudness


def gaussian(rng, dims, spread, limit, pieces=(), dtype=jnp.bfloat16):
    entries = spread * jax.random.normal(rng, dims, jnp.float32)
    if pieces:
        entries = entries * block_scale(rng, dims, pieces, -0.22, 0.18)
    return jnp.clip(entries, -limit, limit).astype(dtype)


def setup_inputs(seed: int = 0) -> dict:
    key_list = jax.random.split(jax.random.key(seed), 7)
    return {
        "gate": gaussian(key_list[0], (TOKENS, FF), 1.0, 6.0, ((0, 4), (1, 64))),
        "upward": gaussian(key_list[1], (TOKENS, FF), 1.0, 6.0, ((0, 4), (1, 64))),
        "cotangent": gaussian(key_list[2], (TOKENS, D), 0.25, 4.0, ((0, 4), (1, 64))),
        "down_weight": gaussian(key_list[3], (FF, D), FF ** -0.5, 0.046875, ((0, 64),)),
        "error_buffer": gaussian(key_list[4], (N_DP, FF, D), 4.0, 24.0, ((0, 4), (1, 64))),
        "start_q": gaussian(key_list[5], (FF, RANK), FF ** -0.5, 0.046875, ((0, 64),), jnp.float32),
    }


def reference(gate, upward, cotangent, down_weight, error_buffer, start_q):
    gate_f = gate.astype(jnp.float32)
    up_f = upward.astype(jnp.float32)
    sigma = jax.nn.sigmoid(gate_f)
    silu = gate_f * sigma
    hidden = (silu * up_f).astype(jnp.bfloat16)
    d_hidden = jnp.dot(cotangent.astype(jnp.float32), down_weight.T.astype(jnp.float32), preferred_element_type=jnp.float32)
    d_gate = (d_hidden * up_f * sigma * (1.0 + gate_f * (1.0 - sigma))).astype(jnp.bfloat16)
    d_up = (d_hidden * silu).astype(jnp.bfloat16)
    grads = []
    basis = jnp.zeros((RANK, D), jnp.float32)
    for group in range(N_DP):
        rows_h = hidden[group * TOK:(group + 1) * TOK]
        rows_c = cotangent[group * TOK:(group + 1) * TOK]
        matrix = error_buffer[group].astype(jnp.float32) + jnp.dot(rows_h.T.astype(jnp.float32), rows_c.astype(jnp.float32), preferred_element_type=jnp.float32)
        grads.append(matrix)
        basis = basis + jnp.dot(start_q.T, matrix, precision=lax.Precision.HIGHEST)
    basis = basis / N_DP
    gram = jnp.dot(basis, basis.T, precision=lax.Precision.HIGHEST)
    lower = jnp.linalg.cholesky(gram)
    basis_hat = lax.linalg.triangular_solve(lower, basis, left_side=True, lower=True)
    next_q = jnp.zeros((FF, RANK), jnp.float32)
    for group in range(N_DP):
        next_q = next_q + jnp.dot(grads[group], basis_hat.T, precision=lax.Precision.HIGHEST)
    next_q = next_q / N_DP
    approx = jnp.dot(next_q, basis_hat, precision=lax.Precision.HIGHEST)
    new_error = jnp.stack([(matrix - approx).astype(jnp.bfloat16) for matrix in grads])
    return (d_gate, d_up, new_error, next_q)
```

```python
import jax
import jax.numpy as jnp
from jax import lax
from jax.sharding import Mesh, PartitionSpec as P

BF = jnp.bfloat16
F32 = jnp.float32
X, Z, CORES = 4, 8, 2
PLANE = ("x", "z", "core")


def dot(a, b):
    return jnp.dot(a, b, preferred_element_type=F32)


def split(a):
    high = a.astype(BF)
    return high, (a - high.astype(F32)).astype(BF)


def spread(a, n):
    return jnp.broadcast_to(a[None], (n,) + a.shape)


def total(a, axis, n):
    return lax.all_to_all(spread(a, n), axis, 0, 0).astype(F32).sum(0)


def local(gate, upward, cotangent, down_weight, error_buffer, start_q):
    groups = lax.axis_size("dp")
    rank = start_q.shape[1]
    error = error_buffer[0]
    piece = lax.all_gather(cotangent, PLANE, axis=1, tiled=True)

    gate_f = gate.T.astype(F32)
    up_f = upward.T.astype(F32)
    sigma = jax.nn.sigmoid(gate_f)
    silu = gate_f * sigma
    hidden = (silu * up_f).astype(BF)

    q_parts = jnp.concatenate(split(start_q.T), axis=0)

    left = dot(q_parts, hidden)
    left = (left[:rank] + left[rank:]).astype(BF)
    swapped = lax.ppermute(left, "core", [(0, 1), (1, 0)])
    left = (left.astype(F32) + swapped.astype(F32)).astype(BF)
    left = total(left, "x", X).astype(BF)
    left = total(left, "z", Z).astype(BF)

    part = dot(q_parts, error)
    part = (part[:rank] + part[rank:]).astype(BF)
    part = part.reshape(rank, X * Z * CORES, -1).transpose(1, 0, 2)
    part = lax.all_to_all(part, PLANE, 0, 0).astype(F32).sum(0)

    mine = (part + dot(left, cotangent)) / groups
    mine = total(mine, "dp", groups).astype(BF)
    basis = lax.all_to_all(spread(mine, X * Z * CORES), PLANE, 0, 0)
    basis = basis.transpose(1, 0, 2).reshape(rank, -1)

    matrix = error.astype(F32) + dot(hidden, piece)
    gram = lax.dot_general(basis, basis, (((1,), (1,)), ((), ())), preferred_element_type=F32)
    lower = jnp.linalg.cholesky(gram)
    inverse = lax.linalg.triangular_solve(lower, jnp.eye(rank, dtype=F32), left_side=True, lower=True)

    turned = lax.dot_general(basis, matrix.astype(BF), (((1,), (1,)), ((), ())), preferred_element_type=F32)
    turned = total(turned, "dp", groups) / groups
    next_qt = jnp.dot(inverse, turned, precision=lax.Precision.HIGHEST)
    factor = jnp.dot(inverse.T, next_qt, precision=lax.Precision.HIGHEST)
    factor = jnp.concatenate(split(factor), axis=0)
    approx = lax.dot_general(factor, jnp.concatenate([basis, basis], axis=0), (((0,), (0,)), ((), ())), preferred_element_type=F32)
    new_error = (matrix - approx).astype(BF)[None]

    d_hidden = lax.dot_general(down_weight, piece, (((1,), (1,)), ((), ())), preferred_element_type=F32)
    d_gate = (d_hidden * up_f * sigma * (1.0 + gate_f * (1.0 - sigma))).astype(BF).T
    d_up = (d_hidden * silu).astype(BF).T
    return (d_gate, d_up, new_error, next_qt.T)


def solution(mesh):
    mesh = Mesh(mesh.devices.reshape(mesh.shape["dp"], X, Z, CORES), ("dp",) + PLANE)
    in_specs = (
        P("dp", PLANE),
        P("dp", PLANE),
        P("dp", PLANE),
        P(PLANE, None),
        P("dp", PLANE, None),
        P(PLANE, None),
    )
    out_specs = (P("dp", PLANE), P("dp", PLANE), P("dp", PLANE, None), P(PLANE, None))
    return jax.shard_map(local, mesh=mesh, in_specs=in_specs, out_specs=out_specs, check_vma=False)
```

```python
import jax
import jax.numpy as jnp
from jax import lax
from jax.experimental import pallas as pl
from jax.experimental.pallas import tpu as pltpu
from jax.sharding import Mesh, PartitionSpec as P

BF = jnp.bfloat16
F32 = jnp.float32
X, Z, CORES = 4, 8, 2
PLANE = ("x", "z", "core")
NT = (((1,), (1,)), ((), ()))
TN = (((0,), (0,)), ((), ()))


def dot(a, b):
    return jnp.dot(a, b, preferred_element_type=F32)


def split(a):
    high = a.astype(BF)
    return high, (a - high.astype(F32)).astype(BF)


def spread(a, n):
    return jnp.broadcast_to(a[None], (n,) + a.shape)


def total(a, axis, n):
    return lax.all_to_all(spread(a, n), axis, 0, 0).astype(F32).sum(0)


def shift(a, axis, step, n):
    return lax.ppermute(a, axis, [(i, (i + step) % n) for i in range(n)])


def piece_kernel(at_ref, own_ref, other_ref, hidden_ref, error_ref, weight_ref, matrix_in, d_in, matrix_ref, d_ref):
    del matrix_in
    first = at_ref[1] == 0
    own, other = own_ref[0], other_ref[0]
    block = jnp.concatenate([jnp.where(first, own, other), jnp.where(first, other, own)], axis=1)
    matrix_ref[...] = error_ref[...].astype(F32) + dot(hidden_ref[...], block)
    term = lax.dot_general(weight_ref[...], block, NT, preferred_element_type=F32)

    @pl.when(pl.program_id(0) == 0)
    def _():
        d_ref[...] = d_in[...] + term

    @pl.when(pl.program_id(0) > 0)
    def _():
        d_ref[...] += term


def add_piece(z, core, own, other, hidden, error, weight, matrix, d_hidden):
    tokens, wide = own.shape[1], own.shape[2]
    rows = hidden.shape[0]
    column = lambda i, at: (0, i * Z + at[0])
    whole = lambda i, at: (0, 0)
    slab = pl.BlockSpec((rows, CORES * wide), column)
    return pl.pallas_call(
        piece_kernel,
        grid_spec=pltpu.PrefetchScalarGridSpec(
            num_scalar_prefetch=1,
            grid=(X,),
            in_specs=[
                pl.BlockSpec((1, tokens, wide), lambda i, at: (i, 0, 0)),
                pl.BlockSpec((1, tokens, wide), lambda i, at: (i, 0, 0)),
                pl.BlockSpec((rows, tokens), whole),
                slab,
                slab,
                pl.BlockSpec(memory_space=pl.ANY),
                pl.BlockSpec((rows, tokens), whole),
            ],
            out_specs=[slab, pl.BlockSpec((rows, tokens), whole)],
        ),
        out_shape=[
            jax.ShapeDtypeStruct(matrix.shape, F32),
            jax.ShapeDtypeStruct(d_hidden.shape, F32),
        ],
        input_output_aliases={6: 0, 7: 1},
        cost_estimate=pl.CostEstimate(flops=4 * rows * tokens * X * CORES * wide, bytes_accessed=6 << 20, transcendentals=0),
        compiler_params=pltpu.CompilerParams(vmem_limit_bytes=24 << 20),
    )(jnp.stack([z, core]), own, other, hidden, error, weight, matrix, d_hidden)


def final_kernel(matrix_ref, factor_ref, basis_ref, out_ref):
    basis = basis_ref[...]
    approx = lax.dot_general(factor_ref[...], jnp.concatenate([basis, basis], axis=0), TN, preferred_element_type=F32)
    out_ref[...] = (matrix_ref[...] - approx).astype(BF)


def finish(matrix, factor, basis):
    rows, columns = matrix.shape
    step = 1024
    block = pl.BlockSpec((rows, step), lambda i: (0, i))
    return pl.pallas_call(
        final_kernel,
        grid=(columns // step,),
        in_specs=[block, pl.BlockSpec(factor.shape, lambda i: (0, 0)), pl.BlockSpec((basis.shape[0], step), lambda i: (0, i))],
        out_specs=block,
        out_shape=jax.ShapeDtypeStruct(matrix.shape, BF),
        cost_estimate=pl.CostEstimate(flops=2 * rows * columns * 64, bytes_accessed=12 << 20, transcendentals=0),
        compiler_params=pltpu.CompilerParams(vmem_limit_bytes=16 << 20),
    )(matrix, factor, basis)


def local(gate, upward, cotangent, down_weight, error_buffer, start_q):
    groups = lax.axis_size("dp")
    z, core = lax.axis_index("z"), lax.axis_index("core")
    rank = start_q.shape[1]
    tokens, wide = cotangent.shape
    error = error_buffer[0]
    rows, columns = error.shape

    pieces = {0: lax.all_to_all(spread(cotangent, X), "x", 0, 0)}

    gate_f = gate.T.astype(F32)
    up_f = upward.T.astype(F32)
    sigma = jax.nn.sigmoid(gate_f)
    silu = gate_f * sigma
    hidden = (silu * up_f).astype(BF)

    q_parts = jnp.concatenate(split(start_q.T), axis=0)

    left = dot(q_parts, hidden)
    left = (left[:rank] + left[rank:]).astype(BF)
    part = dot(q_parts, error)
    part = (part[:rank] + part[rank:]).astype(BF).reshape(rank, X, Z, CORES, wide)
    mine = lax.dynamic_index_in_dim(part, core, 3, False).reshape(rank, -1)
    theirs = lax.dynamic_index_in_dim(part, 1 - core, 3, False).reshape(rank, -1)
    theirs = shift(jnp.concatenate([left, theirs], axis=1), "core", 1, CORES)
    both = jnp.concatenate([left, mine], axis=1).astype(F32) + theirs.astype(F32)
    both = both.astype(BF)

    left, part = both[:, :tokens], both[:, tokens:].reshape(rank, X, Z * wide).transpose(1, 0, 2)
    both = jnp.concatenate([spread(left, X), part], axis=2)
    both = lax.all_to_all(both, "x", 0, 0).astype(F32).sum(0).astype(BF)
    left, part = both[:, :tokens], both[:, tokens:].reshape(rank, Z, wide).transpose(1, 0, 2)
    both = jnp.concatenate([spread(left, Z), part], axis=2)
    both = lax.all_to_all(both, "z", 0, 0).astype(F32).sum(0)
    left, part = both[:, :tokens].astype(BF), both[:, tokens:]

    mine = (part + dot(left, cotangent)) / groups
    mine = total(mine, "dp", groups).astype(BF)
    mine = lax.all_to_all(spread(mine, X * Z), ("x", "z"), 0, 0)
    theirs = shift(mine, "core", 1, CORES)
    first = core == 0
    basis = jnp.stack([jnp.where(first, mine, theirs), jnp.where(first, theirs, mine)], axis=1)
    basis = basis.transpose(2, 0, 1, 3).reshape(rank, columns)

    up, down = pieces[0], pieces[0]
    half = tokens // 2
    for step in range(1, Z // 2):
        up, down = shift(up, "z", 1, Z), shift(down, "z", Z - 1, Z)
        pieces[step], pieces[Z - step] = up, down
    up, down = shift(up[:, :half], "z", 1, Z), shift(down[:, half:], "z", Z - 1, Z)
    pieces[Z // 2] = jnp.concatenate([up, down], axis=1)

    matrix = jnp.zeros((rows, columns), F32)
    d_hidden = jnp.zeros((rows, tokens), F32)
    for step in (0, 1, 7, 2, 6, 3, 5, 4):
        own = pieces[step]
        other = shift(own, "core", 1, CORES)
        matrix, d_hidden = add_piece((z - step) % Z, core, own, other, hidden, error, down_weight, matrix, d_hidden)

    d_gate = (d_hidden * up_f * sigma * (1.0 + gate_f * (1.0 - sigma))).astype(BF).T
    d_up = (d_hidden * silu).astype(BF).T

    turned = lax.dot_general(basis, matrix.astype(BF), NT, preferred_element_type=F32)
    basis, turned = lax.optimization_barrier((basis, turned))
    turned = total(turned, "dp", groups) / groups
    gram = lax.dot_general(basis, basis, NT, preferred_element_type=F32)
    lower = jnp.linalg.cholesky(gram)
    inverse = lax.linalg.triangular_solve(lower, jnp.eye(rank, dtype=F32), left_side=True, lower=True)
    next_qt = jnp.dot(inverse, turned, precision=lax.Precision.HIGHEST)
    factor = jnp.dot(inverse.T, next_qt, precision=lax.Precision.HIGHEST)
    factor = jnp.concatenate(split(factor), axis=0)
    new_error = finish(matrix, factor, basis)[None]
    return (d_gate, d_up, new_error, next_qt.T)


def solution(mesh):
    mesh = Mesh(mesh.devices.reshape(mesh.shape["dp"], X, Z, CORES), ("dp",) + PLANE)
    in_specs = (
        P("dp", PLANE),
        P("dp", PLANE),
        P("dp", PLANE),
        P(PLANE, None),
        P("dp", PLANE, None),
        P(PLANE, None),
    )
    out_specs = (P("dp", PLANE), P("dp", PLANE), P("dp", PLANE, None), P(PLANE, None))
    return jax.shard_map(local, mesh=mesh, in_specs=in_specs, out_specs=out_specs, check_vma=False)
```

```python
import functools

import jax
import jax.numpy as jnp
from jax import lax
from jax.experimental import pallas as pl
from jax.experimental.pallas import tpu as pltpu
from jax.sharding import Mesh, PartitionSpec as P

BF = jnp.bfloat16
F32 = jnp.float32
X, Z, CORES = 4, 8, 2
PLANE = ("x", "z", "core")
LANES = 128
NT = (((1,), (1,)), ((), ()))
TN = (((0,), (0,)), ((), ()))
VMEM = pl.BlockSpec(memory_space=pltpu.VMEM)
ANY = pl.BlockSpec(memory_space=pl.ANY)
HIGHEST = lax.Precision.HIGHEST


def dot(a, b):
    return jnp.dot(a, b, preferred_element_type=F32)


def split(a):
    high = a.astype(BF)
    return high, (a - high.astype(F32)).astype(BF)


def shift(a, axis, step, n):
    return lax.ppermute(a, axis, [(i, (i + step) % n) for i in range(n)])


def exchange(a, axis):
    return lax.all_to_all(a, axis, 0, 0)


def call(kernel, out, scratch=(), ins=None, outs=None, flops=0, moved=0, vmem=24):
    shapes = [jax.ShapeDtypeStruct(s, t) for s, t in out]
    return pl.pallas_call(
        kernel,
        in_specs=ins,
        out_specs=outs if outs is not None else [VMEM] * len(out),
        out_shape=shapes,
        scratch_shapes=list(scratch),
        cost_estimate=pl.CostEstimate(flops=flops, bytes_accessed=moved, transcendentals=0),
        compiler_params=pltpu.CompilerParams(vmem_limit_bytes=vmem << 20),
    )


def column(z, x, wide):
    return pl.multiple_of((x * Z + z) * (CORES * wide), CORES * wide)


def start_kernel(gate_ref, up_ref, q_ref, error_ref, hidden_ref, send_ref, mine_ref, error_buf, sems):
    rank = q_ref.shape[0]
    columns = error_ref.shape[1] // X
    copies = []
    for x in range(X):
        copies.append(pltpu.make_async_copy(error_ref.at[:, pl.ds(x * columns, columns)], error_buf.at[x], sems.at[x]))
        copies[x].start()
    gate = gate_ref[...].astype(F32)
    hidden = (gate * jax.nn.sigmoid(gate) * up_ref[...].astype(F32)).astype(BF)
    hidden_ref[...] = hidden
    high, low = split(q_ref[...])
    both = jnp.concatenate([high, low], axis=0)
    left = dot(both, hidden)
    left = (left[:rank] + left[rank:]).astype(BF)
    blocks = left.shape[1] // LANES
    for b in range(blocks):
        send_ref[b * rank:(b + 1) * rank, :] = left[:, b * LANES:(b + 1) * LANES]
    first = lax.axis_index("core") == 0
    for x in range(X):
        copies[x].wait()
        term = dot(both, error_buf[x])
        term = (term[:rank] + term[rank:]).astype(BF)
        for z in range(Z):
            at = (x * Z + z) * rank
            zero = term[:, (2 * z) * LANES:(2 * z + 1) * LANES]
            one = term[:, (2 * z + 1) * LANES:(2 * z + 2) * LANES]
            mine_ref[at:at + rank, :] = jnp.where(first, zero, one)
            at += blocks * rank
            send_ref[at:at + rank, :] = jnp.where(first, one, zero)


def slice_kernel(groups, terms_ref, cotangent_ref, out_ref):
    rank = out_ref.shape[1]
    terms = terms_ref[0].astype(F32)
    for i in range(1, Z):
        terms = terms + terms_ref[i].astype(F32)
    blocks = cotangent_ref.shape[0] // LANES
    total = terms[blocks * rank:]
    for b in range(blocks):
        total = total + dot(terms[b * rank:(b + 1) * rank].astype(BF), cotangent_ref[b * LANES:(b + 1) * LANES, :])
    total = total / groups
    for g in range(groups):
        out_ref[g] = total


def spread_kernel(terms_ref, out_ref):
    total = terms_ref[0]
    for g in range(1, terms_ref.shape[0]):
        total = total + terms_ref[g]
    total = total.astype(BF)
    for i in range(out_ref.shape[0]):
        out_ref[i] = total


def piece_kernel(steps, *refs):
    n = len(steps)
    own, other = refs[:n], refs[n:2 * n]
    hidden_ref, error_ref, weight_ref, d_in, matrix_ref, d_ref, error_buf, weight_buf, sems = refs[2 * n:]
    tokens, wide = own[0].shape[1:]
    width = CORES * wide
    me = lax.axis_index("z")
    first = lax.axis_index("core") == 0
    copies = []
    for i, step in enumerate(steps):
        for x in range(X):
            at = column(lax.rem(me + (Z - step), Z), x, wide)
            b = i * X + x
            pair = []
            for k, (source, target) in enumerate(((error_ref, error_buf), (weight_ref, weight_buf))):
                pair.append(pltpu.make_async_copy(source.at[:, pl.ds(at, width)], target.at[:, pl.ds(b * width, width)], sems.at[k, b]))
                pair[k].start()
            copies.append(pair)
    hidden = hidden_ref[...]
    total = d_in[...]
    for i in range(n):
        blocks = []
        for x in range(X):
            a, b = own[i][x], other[i][x]
            blocks += [jnp.where(first, a, b), jnp.where(first, b, a)]
            for copy in copies[i * X + x]:
                copy.wait()
        block = jnp.concatenate(blocks, axis=1)
        span = slice(i * X * width, (i + 1) * X * width)
        matrix_ref[:, span] = error_buf[:, span].astype(F32) + dot(hidden, block)
        total = total + lax.dot_general(block, weight_buf[:, span], NT, preferred_element_type=F32)
    d_ref[...] = total


def add_pieces(steps, own, other, hidden, error, weight, d_hidden):
    n = len(steps)
    tokens, wide = own[0].shape[1:]
    rows = hidden.shape[0]
    columns = n * X * CORES * wide
    return call(
        functools.partial(piece_kernel, steps),
        [((rows, columns), F32), ((tokens, rows), F32)],
        [pltpu.VMEM((rows, columns), BF), pltpu.VMEM((rows, columns), BF), pltpu.SemaphoreType.DMA((2, n * X))],
        [VMEM] * (2 * n + 1) + [ANY, ANY, VMEM],
        flops=4 * rows * tokens * columns,
        moved=4 * rows * columns,
    )(*own, *other, hidden, error, weight, d_hidden)


def basis_block(first, me, step, x, mine_ref, theirs_ref):
    at = x * Z + lax.rem(me + (Z - step), Z)
    a, b = mine_ref[at], theirs_ref[at]
    return jnp.concatenate([jnp.where(first, a, b), jnp.where(first, b, a)], axis=1)


def turn_kernel(layout, groups, *refs):
    n = len(layout)
    mine_ref, theirs_ref, out_ref, gram_ref = refs[n:]
    me = lax.axis_index("z")
    first = lax.axis_index("core") == 0
    total, gram = 0.0, 0.0
    for matrix_ref, steps in zip(refs[:n], layout):
        for i, step in enumerate(steps):
            basis = jnp.concatenate([basis_block(first, me, step, x, mine_ref, theirs_ref) for x in range(X)], axis=1)
            span = slice(i * basis.shape[1], (i + 1) * basis.shape[1])
            total = total + lax.dot_general(matrix_ref[:, span].astype(BF), basis, NT, preferred_element_type=F32)
            gram = gram + lax.dot_general(basis, basis, NT, preferred_element_type=F32)
    gram_ref[...] = gram
    total = total.T
    for g in range(groups):
        out_ref[g] = total


def final_kernel(layout, groups, *refs):
    n = len(layout)
    mine_ref, theirs_ref, terms_ref, inverse_ref, out_ref, q_ref, buf, sems = refs[n:]
    wide = mine_ref.shape[2]
    width = CORES * wide
    me = lax.axis_index("z")
    first = lax.axis_index("core") == 0
    total = terms_ref[0]
    for g in range(1, groups):
        total = total + terms_ref[g]
    inverse = inverse_ref[...]
    next_q = jnp.dot(inverse, total / groups, precision=HIGHEST, preferred_element_type=F32)
    q_ref[...] = next_q
    factor = lax.dot_general(inverse, next_q, TN, precision=HIGHEST, preferred_element_type=F32)
    high, low = split(factor.T)
    factor = jnp.concatenate([high, low], axis=1)
    copies = []
    for matrix_ref, steps in zip(refs[:n], layout):
        for i, step in enumerate(steps):
            basis = jnp.concatenate([basis_block(first, me, step, x, mine_ref, theirs_ref) for x in range(X)], axis=1)
            basis = jnp.concatenate([basis, basis], axis=0)
            span = slice(i * X * width, (i + 1) * X * width)
            buf[step] = (matrix_ref[:, span] - dot(factor, basis)).astype(BF)
            for x in range(X):
                at = column(lax.rem(me + (Z - step), Z), x, wide)
                copy = pltpu.make_async_copy(buf.at[step, :, pl.ds(x * width, width)], out_ref.at[:, pl.ds(at, width)], sems.at[step, x])
                copy.start()
                copies.append(copy)
    for copy in copies:
        copy.wait()


def local(gate, upward, cotangent, down_weight, error_buffer, start_q):
    groups = lax.axis_size("dp")
    rank = start_q.shape[1]
    tokens, wide = cotangent.shape
    error = error_buffer[0]
    rows, columns = error.shape
    tiles = tokens // LANES * rank

    hidden, send, mine = call(
        start_kernel,
        [((rows, tokens), BF), ((tiles + X * Z * rank, wide), BF), ((X * Z * rank, wide), BF)],
        [pltpu.VMEM((X, rows, columns // X), BF), pltpu.SemaphoreType.DMA((X,))],
        [VMEM, VMEM, VMEM, ANY],
        flops=4 * rows * rank * columns,
        moved=2 * rows * columns,
    )(gate.T, upward.T, start_q.T, error)
    theirs = shift(send, "core", 1, CORES)
    left = (send[:tiles].astype(F32) + theirs[:tiles].astype(F32)).astype(BF)
    part = (mine.astype(F32) + theirs[tiles:].astype(F32)).astype(BF).reshape(X, Z * rank, wide)

    spread = lambda a, n: jnp.broadcast_to(a[None], (n,) + a.shape)
    got = exchange(jnp.concatenate([spread(cotangent, X), spread(left, X), part], axis=1), "x")
    pieces, others = {0: got[:, :tokens]}, {}
    sums = got[:, tokens:].astype(F32).sum(0).astype(BF)
    terms = jnp.concatenate([spread(sums[:tiles], Z), sums[tiles:].reshape(Z, rank, wide)], axis=1)

    def ring(step):
        pieces[step] = shift(pieces[step - 1], "z", 1, Z)
        pieces[Z - step] = shift(pieces[(Z - step + 1) % Z], "z", Z - 1, Z)

    def swap(*steps):
        for step in steps:
            others[step] = shift(pieces[step], "core", 1, CORES)

    matrices, layout = [], []

    def use(steps, d_hidden):
        matrix, d_hidden = add_pieces(steps, [pieces[s] for s in steps], [others[s] for s in steps], hidden, error, down_weight, d_hidden)
        matrices.append(matrix)
        layout.append(steps)
        return d_hidden

    d_hidden = jnp.zeros((tokens, rows), F32)
    ring(1)
    swap(0)
    terms = exchange(terms, "z")
    d_hidden = use((0,), d_hidden)
    terms, pieces[1], pieces[7], d_hidden = lax.optimization_barrier((terms, pieces[1], pieces[7], d_hidden))
    ring(2)
    swap(1, 7)
    terms, = call(functools.partial(slice_kernel, groups), [((groups, rank, wide), F32)], ins=[VMEM, VMEM])(terms, cotangent)
    terms = exchange(terms, "dp")
    d_hidden = use((1, 7), d_hidden)
    terms, pieces[2], pieces[6], d_hidden = lax.optimization_barrier((terms, pieces[2], pieces[6], d_hidden))
    ring(3)
    swap(2, 6)
    mine, = call(spread_kernel, [((X * Z, rank, wide), BF)], ins=[VMEM])(terms)
    mine = exchange(mine, ("x", "z"))
    d_hidden = use((2, 6), d_hidden)
    pieces[3], pieces[5], d_hidden = lax.optimization_barrier((pieces[3], pieces[5], d_hidden))
    half = tokens // 2
    up = shift(pieces[3][:, :half], "z", 1, Z)
    down = shift(pieces[5][:, half:], "z", Z - 1, Z)
    swap(3, 5)
    d_hidden = use((3, 5), d_hidden)
    pieces[4] = jnp.concatenate([up, down], axis=1)
    swap(4)
    d_hidden = use((4,), d_hidden)
    theirs = shift(mine, "core", 1, CORES)

    terms, gram = call(
        functools.partial(turn_kernel, tuple(layout), groups),
        [((groups, rank, rows), F32), ((rank, rank), F32)],
        ins=[VMEM] * (len(layout) + 2),
        flops=2 * rows * rank * columns,
        moved=4 * rows * columns,
    )(*matrices, mine, theirs)
    terms = exchange(terms, "dp")
    lower = jnp.linalg.cholesky(gram)
    inverse = lax.linalg.triangular_solve(lower, jnp.eye(rank, dtype=F32), left_side=True, lower=True)

    d_hidden = d_hidden.T
    gate_f = gate.T.astype(F32)
    up_f = upward.T.astype(F32)
    sigma = jax.nn.sigmoid(gate_f)
    d_gate = (d_hidden * up_f * sigma * (1.0 + gate_f * (1.0 - sigma))).astype(BF).T
    d_up = (d_hidden * (gate_f * sigma)).astype(BF).T

    new_error, next_q = call(
        functools.partial(final_kernel, tuple(layout), groups),
        [((rows, columns), BF), ((rank, rows), F32)],
        [pltpu.VMEM((Z, rows, columns // Z), BF), pltpu.SemaphoreType.DMA((Z, X))],
        [VMEM] * (len(layout) + 4),
        [ANY, VMEM],
        flops=4 * rows * rank * columns,
        moved=6 * rows * columns,
    )(*matrices, mine, theirs, terms, inverse)
    return (d_gate, d_up, new_error[None], next_q.T)


def solution(mesh):
    mesh = Mesh(mesh.devices.reshape(mesh.shape["dp"], X, Z, CORES), ("dp",) + PLANE)
    in_specs = (
        P("dp", PLANE),
        P("dp", PLANE),
        P("dp", PLANE),
        P(PLANE, None),
        P("dp", PLANE, None),
        P(PLANE, None),
    )
    out_specs = (P("dp", PLANE), P("dp", PLANE), P("dp", PLANE, None), P(PLANE, None))
    return jax.shard_map(local, mesh=mesh, in_specs=in_specs, out_specs=out_specs, check_vma=False)
```

```python
import functools

import jax
import jax.numpy as jnp
from jax import lax
from jax.experimental import pallas as pl
from jax.experimental.pallas import tpu as pltpu
from jax.sharding import Mesh, PartitionSpec as P

BF = jnp.bfloat16
F32 = jnp.float32
X, Z, CORES = 4, 8, 2
PLANE = ("x", "z", "core")
LANES = 128
NT = (((1,), (1,)), ((), ()))
TN = (((0,), (0,)), ((), ()))
VMEM = pl.BlockSpec(memory_space=pltpu.VMEM)
HBM = pl.BlockSpec(memory_space=pltpu.HBM)
HIGHEST = lax.Precision.HIGHEST


def dot(a, b):
    return jnp.dot(a, b, preferred_element_type=F32)


def split(a):
    high = a.astype(BF)
    return high, (a - high.astype(F32)).astype(BF)


def shift(a, axis, step, n):
    return lax.ppermute(a, axis, [(i, (i + step) % n) for i in range(n)])


def exchange(a, axis):
    return lax.all_to_all(a, axis, 0, 0)


def call(kernel, out, scratch=(), ins=None, outs=None, flops=0, moved=0, vmem=16):
    outs = outs if outs is not None else [VMEM] * len(out)
    run = pl.pallas_call(
        kernel,
        in_specs=[VMEM if spec is None else spec for spec in ins],
        out_specs=[VMEM if spec is None else spec for spec in outs],
        out_shape=[jax.ShapeDtypeStruct(s, t) if spec is None else spec.memory_space(s, t) for spec, (s, t) in zip(outs, out)],
        scratch_shapes=list(scratch),
        cost_estimate=pl.CostEstimate(flops=flops, bytes_accessed=moved, transcendentals=0),
        compiler_params=pltpu.CompilerParams(vmem_limit_bytes=vmem << 20),
    )

    def placed(a, spec):
        return a if spec is None else pltpu.with_memory_space_constraint(a, spec.memory_space)

    return lambda *args: run(*(placed(a, spec) for a, spec in zip(args, ins)))


def back(axis, step, n):
    return lax.rem(lax.axis_index(axis) + (n - step), n)


def column(step, hop, wide):
    chip = back("x", hop, X) * Z + back("z", step, Z)
    return pl.multiple_of(chip * (CORES * wide), CORES * wide)


def fetch(source, target, sem):
    copy = pltpu.make_async_copy(source, target, sem)
    copy.start()
    return copy


def start_kernel(gate_hbm, up_hbm, q_hbm, error_ref, hidden_ref, send_ref, mine_ref, gate_ref, up_ref, q_ref, error_buf, sems):
    rank = q_ref.shape[0]
    columns = error_ref.shape[1] // X
    small = [fetch(a, b, sems.at[X + i]) for i, (a, b) in enumerate(((gate_hbm, gate_ref), (up_hbm, up_ref), (q_hbm, q_ref)))]
    copies = [fetch(error_ref.at[:, pl.ds(x * columns, columns)], error_buf.at[x], sems.at[x]) for x in range(X)]
    for copy in small:
        copy.wait()
    gate = gate_ref[...].astype(F32)
    hidden = (gate * jax.nn.sigmoid(gate) * up_ref[...].astype(F32)).astype(BF)
    hidden_ref[...] = hidden
    high, low = split(q_ref[...])
    both = jnp.concatenate([high, low], axis=0)
    left = dot(both, hidden)
    left = (left[:rank] + left[rank:]).astype(BF)
    blocks = left.shape[1] // LANES
    for b in range(blocks):
        send_ref[b * rank:(b + 1) * rank, :] = left[:, b * LANES:(b + 1) * LANES]
    first = lax.axis_index("core") == 0
    for x in range(X):
        copies[x].wait()
        term = dot(both, error_buf[x])
        term = (term[:rank] + term[rank:]).astype(BF)
        for z in range(Z):
            at = (x * Z + z) * rank
            zero = term[:, (2 * z) * LANES:(2 * z + 1) * LANES]
            one = term[:, (2 * z + 1) * LANES:(2 * z + 2) * LANES]
            mine_ref[at:at + rank, :] = jnp.where(first, zero, one)
            at += blocks * rank
            send_ref[at:at + rank, :] = jnp.where(first, one, zero)


def pack_kernel(send_ref, theirs_ref, mine_ref, out_ref):
    tiles = send_ref.shape[0] - mine_ref.shape[0]
    left = (send_ref[:tiles, :].astype(F32) + theirs_ref[:tiles, :].astype(F32)).astype(BF)
    part = (mine_ref[...].astype(F32) + theirs_ref[tiles:, :].astype(F32)).astype(BF)
    size = part.shape[0] // X
    for x in range(X):
        out_ref[x, :tiles, :] = left
        out_ref[x, tiles:, :] = part[x * size:(x + 1) * size]


def repack_kernel(terms_ref, out_ref):
    total = terms_ref[0].astype(F32)
    for x in range(1, X):
        total = total + terms_ref[x].astype(F32)
    total = total.astype(BF)
    rank = (terms_ref.shape[1] - out_ref.shape[1]) // (Z - 1)
    tiles = out_ref.shape[1] - rank
    for z in range(Z):
        out_ref[z, :tiles, :] = total[:tiles]
        out_ref[z, tiles:, :] = total[tiles + z * rank:tiles + (z + 1) * rank]


def slice_kernel(groups, terms_ref, cotangent_ref, out_ref):
    rank = out_ref.shape[1]
    terms = terms_ref[0].astype(F32)
    for i in range(1, Z):
        terms = terms + terms_ref[i].astype(F32)
    blocks = cotangent_ref.shape[0] // LANES
    total = terms[blocks * rank:]
    for b in range(blocks):
        total = total + dot(terms[b * rank:(b + 1) * rank].astype(BF), cotangent_ref[b * LANES:(b + 1) * LANES, :])
    total = total / groups
    for g in range(groups):
        out_ref[g] = total


def spread_kernel(terms_ref, out_ref):
    total = terms_ref[0]
    for g in range(1, terms_ref.shape[0]):
        total = total + terms_ref[g]
    total = total.astype(BF)
    for i in range(out_ref.shape[0]):
        out_ref[i] = total


def piece_kernel(steps, last, *refs):
    n = len(steps)
    own, other = refs[:n], refs[n:2 * n]
    refs = refs[2 * n:]
    hidden_ref, error_ref, weight_ref, d_in = refs[:4]
    refs = refs[4:]
    if last:
        gate_hbm, up_hbm, matrix_ref, d_gate_ref, d_up_ref, error_buf, weight_buf, sems, gate_ref, up_ref, pair_sems = refs
        pair = [fetch(gate_hbm, gate_ref, pair_sems.at[0]), fetch(up_hbm, up_ref, pair_sems.at[1])]
    else:
        matrix_ref, d_ref, error_buf, weight_buf, sems = refs
    wide = own[0].shape[2]
    width = CORES * wide
    first = lax.axis_index("core") == 0
    copies = []
    for i, step in enumerate(steps):
        for hop in range(X):
            at = column(step, hop, wide)
            b = i * X + hop
            for k, (source, target) in enumerate(((error_ref, error_buf), (weight_ref, weight_buf))):
                copies.append(fetch(source.at[:, pl.ds(at, width)], target.at[:, pl.ds(b * width, width)], sems.at[k, b]))
    hidden = hidden_ref[...]
    total = d_in[...]
    for i in range(n):
        blocks = []
        for hop in range(X):
            a, b = own[i][hop], other[i][hop]
            blocks += [jnp.where(first, a, b), jnp.where(first, b, a)]
        for copy in copies[2 * X * i:2 * X * (i + 1)]:
            copy.wait()
        block = jnp.concatenate(blocks, axis=1)
        span = slice(i * X * width, (i + 1) * X * width)
        matrix_ref[:, span] = error_buf[:, span].astype(F32) + dot(hidden, block)
        total = total + lax.dot_general(block, weight_buf[:, span], NT, preferred_element_type=F32)
    if not last:
        d_ref[...] = total
        return
    for copy in pair:
        copy.wait()
    total = total.T
    gate = gate_ref[...].astype(F32)
    sigma = jax.nn.sigmoid(gate)
    d_gate_ref[...] = (total * up_ref[...].astype(F32) * sigma * (1.0 + gate * (1.0 - sigma))).astype(BF)
    d_up_ref[...] = (total * (gate * sigma)).astype(BF)


def add_pieces(steps, own, other, hidden, error, weight, d_hidden, gate=None, upward=None):
    n = len(steps)
    tokens, wide = own[0].shape[1:]
    rows = hidden.shape[0]
    columns = n * X * CORES * wide
    last = gate is not None
    scratch = [pltpu.VMEM((rows, columns), BF), pltpu.VMEM((rows, columns), BF), pltpu.SemaphoreType.DMA((2, n * X))]
    if last:
        scratch += [pltpu.VMEM((rows, tokens), BF), pltpu.VMEM((rows, tokens), BF), pltpu.SemaphoreType.DMA((2,))]
    return call(
        functools.partial(piece_kernel, steps, last),
        [((rows, columns), F32)] + ([((rows, tokens), BF)] * 2 if last else [((tokens, rows), F32)]),
        scratch,
        [VMEM] * (2 * n + 1) + [HBM, HBM, VMEM] + [HBM, HBM] * last,
        [VMEM, None, None] if last else None,
        flops=4 * rows * tokens * columns,
        moved=4 * rows * columns,
    )(*own, *other, hidden, error, weight, d_hidden, *([gate, upward] if last else []))


def basis_block(first, step, hop, mine_ref, theirs_ref):
    at = back("x", hop, X) * Z + back("z", step, Z)
    a, b = mine_ref[at], theirs_ref[at]
    return jnp.concatenate([jnp.where(first, a, b), jnp.where(first, b, a)], axis=1)


def turn_kernel(layout, groups, *refs):
    n = len(layout)
    mine_ref, theirs_ref, out_ref, gram_ref = refs[n:]
    first = lax.axis_index("core") == 0
    total, gram = 0.0, 0.0
    for matrix_ref, steps in zip(refs[:n], layout):
        for i, step in enumerate(steps):
            basis = jnp.concatenate([basis_block(first, step, hop, mine_ref, theirs_ref) for hop in range(X)], axis=1)
            span = slice(i * basis.shape[1], (i + 1) * basis.shape[1])
            total = total + lax.dot_general(matrix_ref[:, span].astype(BF), basis, NT, preferred_element_type=F32)
            gram = gram + lax.dot_general(basis, basis, NT, preferred_element_type=F32)
    gram_ref[...] = gram
    total = total.T
    for g in range(groups):
        out_ref[g] = total


def inverse_kernel(gram_ref, out_ref):
    n = gram_ref.shape[0]
    row = lax.broadcasted_iota(jnp.int32, (n, 2 * n), 0)
    col = lax.broadcasted_iota(jnp.int32, (n, 2 * n), 1)
    both = jnp.concatenate([gram_ref[...], jnp.zeros((n, n), F32)], axis=1) + jnp.where(col == row + n, 1.0, 0.0)
    for k in range(n):
        pivot = both[k:k + 1, k:k + 1]
        scaled = both[k:k + 1, :] * lax.rsqrt(pivot)
        column_k = both[:, k:k + 1] * lax.rsqrt(pivot)
        both = jnp.where(row > k, both - column_k * scaled, jnp.where(row == k, scaled, both))
    out_ref[...] = both[:, n:]


def final_kernel(layout, groups, *refs):
    n = len(layout)
    mine_ref, theirs_ref, terms_ref, inverse_ref, out_ref, q_ref, buf, sems = refs[n:]
    wide = mine_ref.shape[2]
    width = CORES * wide
    first = lax.axis_index("core") == 0
    total = terms_ref[0]
    for g in range(1, groups):
        total = total + terms_ref[g]
    inverse = inverse_ref[...]
    next_q = jnp.dot(inverse, total / groups, precision=HIGHEST, preferred_element_type=F32)
    q_ref[...] = next_q
    factor = lax.dot_general(inverse, next_q, TN, precision=HIGHEST, preferred_element_type=F32)
    high, low = split(factor.T)
    factor = jnp.concatenate([high, low], axis=1)
    copies = []
    for matrix_ref, steps in zip(refs[:n], layout):
        for i, step in enumerate(steps):
            basis = jnp.concatenate([basis_block(first, step, hop, mine_ref, theirs_ref) for hop in range(X)], axis=1)
            basis = jnp.concatenate([basis, basis], axis=0)
            span = slice(i * X * width, (i + 1) * X * width)
            buf[step] = (matrix_ref[:, span] - dot(factor, basis)).astype(BF)
            for x in range(X):
                at = column(step, x, wide)
                copies.append(fetch(buf.at[step, :, pl.ds(x * width, width)], out_ref.at[:, pl.ds(at, width)], sems.at[step, x]))
    for copy in copies:
        copy.wait()


def local(gate, upward, cotangent, down_weight, error_buffer, start_q):
    groups = lax.axis_size("dp")
    rank = start_q.shape[1]
    tokens, wide = cotangent.shape
    error = error_buffer[0]
    rows, columns = error.shape
    tiles = tokens // LANES * rank

    blocks = [cotangent] + [shift(cotangent, "x", hop, X) for hop in range(1, X)]
    pieces, others = {0: jnp.stack(blocks)}, {}

    hidden, send, mine = call(
        start_kernel,
        [((rows, tokens), BF), ((tiles + X * Z * rank, wide), BF), ((X * Z * rank, wide), BF)],
        [
            pltpu.VMEM((rows, tokens), BF),
            pltpu.VMEM((rows, tokens), BF),
            pltpu.VMEM((rank, rows), F32),
            pltpu.VMEM((X, rows, columns // X), BF),
            pltpu.SemaphoreType.DMA((X + 3,)),
        ],
        [HBM, HBM, HBM, HBM],
        flops=4 * rows * rank * columns,
        moved=2 * rows * columns,
    )(gate.T, upward.T, start_q.T, error)
    theirs = shift(send, "core", 1, CORES)
    terms, = call(pack_kernel, [((X, tiles + Z * rank, wide), BF)], ins=[VMEM] * 3)(send, theirs, mine)

    def ring(step):
        pieces[step] = shift(pieces[step - 1], "z", 1, Z)
        pieces[Z - step] = shift(pieces[(Z - step + 1) % Z], "z", Z - 1, Z)

    def swap(*steps):
        for step in steps:
            others[step] = shift(pieces[step], "core", 1, CORES)

    matrices, layout = [], []

    def use(steps, d_hidden, *more):
        matrix, *rest = add_pieces(steps, [pieces[s] for s in steps], [others[s] for s in steps], hidden, error, down_weight, d_hidden, *more)
        matrices.append(matrix)
        layout.append(steps)
        return rest if more else rest[0]

    d_hidden = jnp.zeros((tokens, rows), F32)
    ring(1)
    swap(0)
    terms = exchange(terms, "x")
    terms, pieces[1], pieces[7] = lax.optimization_barrier((terms, pieces[1], pieces[7]))
    ring(2)
    swap(1, 7)
    terms, = call(repack_kernel, [((Z, tiles + rank, wide), BF)], ins=[VMEM])(terms)
    terms = exchange(terms, "z")
    d_hidden = use((0,), d_hidden)
    terms, pieces[2], pieces[6], d_hidden = lax.optimization_barrier((terms, pieces[2], pieces[6], d_hidden))
    ring(3)
    swap(2, 6)
    terms, = call(functools.partial(slice_kernel, groups), [((groups, rank, wide), F32)], ins=[VMEM, None])(terms, cotangent)
    terms = exchange(terms, "dp")
    d_hidden = use((1, 7), d_hidden)
    terms, pieces[3], pieces[5], d_hidden = lax.optimization_barrier((terms, pieces[3], pieces[5], d_hidden))
    half = tokens // 2
    up = shift(pieces[3][:, :half], "z", 1, Z)
    down = shift(pieces[5][:, half:], "z", Z - 1, Z)
    swap(3, 5)
    mine, = call(spread_kernel, [((X * Z, rank, wide), BF)], ins=[VMEM])(terms)
    mine = exchange(mine, ("x", "z"))
    d_hidden = use((2, 6), d_hidden)
    pieces[4] = jnp.concatenate([up, down], axis=1)
    swap(4)
    mine, d_hidden = lax.optimization_barrier((mine, d_hidden))
    theirs = shift(mine, "core", 1, CORES)
    d_hidden = use((3, 5), d_hidden)
    d_gate, d_up = use((4,), d_hidden, gate.T, upward.T)

    terms, gram = call(
        functools.partial(turn_kernel, tuple(layout), groups),
        [((groups, rank, rows), F32), ((rank, rank), F32)],
        ins=[VMEM] * (len(layout) + 2),
        flops=2 * rows * rank * columns,
        moved=4 * rows * columns,
    )(*matrices, mine, theirs)
    terms = exchange(terms, "dp")
    inverse, = call(inverse_kernel, [((rank, rank), F32)], ins=[VMEM])(gram)

    new_error, next_q = call(
        functools.partial(final_kernel, tuple(layout), groups),
        [((rows, columns), BF), ((rank, rows), F32)],
        [pltpu.VMEM((Z, rows, columns // Z), BF), pltpu.SemaphoreType.DMA((Z, X))],
        [VMEM] * (len(layout) + 4),
        [HBM, None],
        flops=4 * rows * rank * columns,
        moved=6 * rows * columns,
    )(*matrices, mine, theirs, terms, inverse)
    return (d_gate.T, d_up.T, new_error[None], next_q.T)


def solution(mesh):
    mesh = Mesh(mesh.devices.reshape(mesh.shape["dp"], X, Z, CORES), ("dp",) + PLANE)
    in_specs = (
        P("dp", PLANE),
        P("dp", PLANE),
        P("dp", PLANE),
        P(PLANE, None),
        P("dp", PLANE, None),
        P(PLANE, None),
    )
    out_specs = (P("dp", PLANE), P("dp", PLANE), P("dp", PLANE, None), P(PLANE, None))
    return jax.shard_map(local, mesh=mesh, in_specs=in_specs, out_specs=out_specs, check_vma=False)
```

```python
import functools

import jax
import jax.numpy as jnp
from jax import lax
from jax.experimental import pallas as pl
from jax.experimental.pallas import tpu as pltpu
from jax.sharding import Mesh, PartitionSpec as P

BF = jnp.bfloat16
F32 = jnp.float32
X, Z, CORES = 4, 8, 2
PLANE = ("x", "z", "core")
LANES = 128
NT = (((1,), (1,)), ((), ()))
TN = (((0,), (0,)), ((), ()))
VMEM = pl.BlockSpec(memory_space=pltpu.VMEM)
HBM = pl.BlockSpec(memory_space=pltpu.HBM)
HIGHEST = lax.Precision.HIGHEST


def dot(a, b):
    return jnp.dot(a, b, preferred_element_type=F32)


def split(a):
    high = a.astype(BF)
    return high, (a - high.astype(F32)).astype(BF)


def shift(a, axis, step, n):
    return lax.ppermute(a, axis, [(i, (i + step) % n) for i in range(n)])


def exchange(a, axis):
    return lax.all_to_all(a, axis, 0, 0)


def call(kernel, out, scratch=(), ins=None, outs=None, flops=0, moved=0, vmem=16):
    outs = outs if outs is not None else [VMEM] * len(out)
    run = pl.pallas_call(
        kernel,
        in_specs=[VMEM if spec is None else spec for spec in ins],
        out_specs=[VMEM if spec is None else spec for spec in outs],
        out_shape=[jax.ShapeDtypeStruct(s, t) if spec is None else spec.memory_space(s, t) for spec, (s, t) in zip(outs, out)],
        scratch_shapes=list(scratch),
        cost_estimate=pl.CostEstimate(flops=flops, bytes_accessed=moved, transcendentals=0),
        compiler_params=pltpu.CompilerParams(vmem_limit_bytes=vmem << 20),
    )

    def placed(a, spec):
        return a if spec is None else pltpu.with_memory_space_constraint(a, spec.memory_space)

    return lambda *args: run(*(placed(a, spec) for a, spec in zip(args, ins)))


def back(axis, step, n):
    return lax.rem(lax.axis_index(axis) + (n - step), n)


def columns_of(step, hop, wide):
    chip = back("x", hop, X) * Z + back("z", step, Z)
    core = lax.axis_index("core")
    return [pl.multiple_of((chip * CORES + c) * wide, wide) for c in (core, 1 - core)]


def slabs(ref, step, wide):
    return jnp.concatenate([ref[:, pl.ds(at, wide)] for hop in range(X) for at in columns_of(step, hop, wide)], axis=1)


def fetch(source, target, sem):
    copy = pltpu.make_async_copy(source, target, sem)
    copy.start()
    return copy


def start_kernel(gate_hbm, up_hbm, q_hbm, error_ref, hidden_ref, send_ref, mine_ref, error_buf, gate_ref, up_ref, q_ref, sems):
    rank = q_ref.shape[0]
    columns = error_ref.shape[1] // X
    small = [fetch(a, b, sems.at[X + i]) for i, (a, b) in enumerate(((gate_hbm, gate_ref), (up_hbm, up_ref), (q_hbm, q_ref)))]
    spans = [slice(x * columns, (x + 1) * columns) for x in range(X)]
    copies = [fetch(error_ref.at[:, spans[x]], error_buf.at[:, spans[x]], sems.at[x]) for x in range(X)]
    for copy in small:
        copy.wait()
    gate = gate_ref[...].astype(F32)
    hidden = (gate * jax.nn.sigmoid(gate) * up_ref[...].astype(F32)).astype(BF)
    hidden_ref[...] = hidden
    high, low = split(q_ref[...])
    both = jnp.concatenate([high, low], axis=0)
    left = dot(both, hidden)
    left = (left[:rank] + left[rank:]).astype(BF)
    blocks = left.shape[1] // LANES
    for b in range(blocks):
        send_ref[b * rank:(b + 1) * rank, :] = left[:, b * LANES:(b + 1) * LANES]
    first = lax.axis_index("core") == 0
    for x in range(X):
        copies[x].wait()
        term = dot(both, error_buf[:, spans[x]])
        term = (term[:rank] + term[rank:]).astype(BF)
        for z in range(Z):
            at = (x * Z + z) * rank
            zero = term[:, (2 * z) * LANES:(2 * z + 1) * LANES]
            one = term[:, (2 * z + 1) * LANES:(2 * z + 2) * LANES]
            mine_ref[at:at + rank, :] = jnp.where(first, zero, one)
            at += blocks * rank
            send_ref[at:at + rank, :] = jnp.where(first, one, zero)


def stack_kernel(*refs):
    for i, ref in enumerate(refs[:-1]):
        refs[-1][i] = ref[...]


def pack_kernel(send_ref, theirs_ref, mine_ref, out_ref):
    tiles = send_ref.shape[0] - mine_ref.shape[0]
    left = (send_ref[:tiles, :].astype(F32) + theirs_ref[:tiles, :].astype(F32)).astype(BF)
    part = (mine_ref[...].astype(F32) + theirs_ref[tiles:, :].astype(F32)).astype(BF)
    size = part.shape[0] // X
    for x in range(X):
        out_ref[x, :tiles, :] = left
        out_ref[x, tiles:, :] = part[x * size:(x + 1) * size]


def repack_kernel(terms_ref, out_ref):
    total = terms_ref[0].astype(F32)
    for x in range(1, X):
        total = total + terms_ref[x].astype(F32)
    total = total.astype(BF)
    rank = (terms_ref.shape[1] - out_ref.shape[1]) // (Z - 1)
    tiles = out_ref.shape[1] - rank
    for z in range(Z):
        out_ref[z, :tiles, :] = total[:tiles]
        out_ref[z, tiles:, :] = total[tiles + z * rank:tiles + (z + 1) * rank]


def slice_kernel(groups, terms_ref, cotangent_ref, out_ref):
    rank = out_ref.shape[1]
    terms = terms_ref[0].astype(F32)
    for i in range(1, Z):
        terms = terms + terms_ref[i].astype(F32)
    blocks = cotangent_ref.shape[0] // LANES
    total = terms[blocks * rank:]
    for b in range(blocks):
        total = total + dot(terms[b * rank:(b + 1) * rank].astype(BF), cotangent_ref[b * LANES:(b + 1) * LANES, :])
    total = total / groups
    for g in range(groups):
        out_ref[g] = total


def spread_kernel(terms_ref, out_ref):
    total = terms_ref[0]
    for g in range(1, terms_ref.shape[0]):
        total = total + terms_ref[g]
    total = total.astype(BF)
    for i in range(out_ref.shape[0]):
        out_ref[i] = total


def piece_kernel(steps, first, last, *refs):
    n = len(steps)
    own, other = refs[:n], refs[n:2 * n]
    refs = refs[2 * n:]
    if first:
        hidden_ref, error_ref, weight_hbm, matrix_ref, d_ref, weight_ref, sem = refs
        copy = fetch(weight_hbm, weight_ref, sem.at[0])
    elif last:
        hidden_ref, error_ref, weight_ref, d_in, gate_hbm, up_hbm, matrix_ref, d_gate_ref, d_up_ref, gate_ref, up_ref, sem = refs
        pair = [fetch(gate_hbm, gate_ref, sem.at[0]), fetch(up_hbm, up_ref, sem.at[1])]
    else:
        hidden_ref, error_ref, weight_ref, d_in, matrix_ref, d_ref = refs
    wide = own[0].shape[2]
    blocks = [jnp.concatenate([ref[hop] for hop in range(X) for ref in (own[i], other[i])], axis=1) for i in range(n)]
    width = blocks[0].shape[1]
    for i, step in enumerate(steps):
        matrix_ref[:, i * width:(i + 1) * width] = slabs(error_ref, step, wide).astype(F32) + dot(hidden_ref[...], blocks[i])
    if first:
        copy.wait()
    block = jnp.concatenate(blocks, axis=1)
    weight = jnp.concatenate([slabs(weight_ref, step, wide) for step in steps], axis=1)
    total = lax.dot_general(block, weight, NT, preferred_element_type=F32)
    if not first:
        total = total + d_in[...]
    if not last:
        d_ref[...] = total
        return
    for copy in pair:
        copy.wait()
    total = total.T
    gate = gate_ref[...].astype(F32)
    sigma = jax.nn.sigmoid(gate)
    d_gate_ref[...] = (total * up_ref[...].astype(F32) * sigma * (1.0 + gate * (1.0 - sigma))).astype(BF)
    d_up_ref[...] = (total * (gate * sigma)).astype(BF)


def add_pieces(steps, own, other, hidden, error, weight, d_hidden, gate=None, upward=None):
    n = len(steps)
    tokens, wide = own[0].shape[1:]
    rows = hidden.shape[0]
    columns = n * X * CORES * wide
    first, last = d_hidden is None, gate is not None
    out = [((rows, columns), F32)]
    scratch, outs, ins = [], None, [VMEM] * (2 * n + 2)
    if last:
        out += [((rows, tokens), BF)] * 2
        outs = [VMEM, None, None]
        ins += [VMEM, VMEM, HBM, HBM]
        scratch = [pltpu.VMEM((rows, tokens), BF), pltpu.VMEM((rows, tokens), BF), pltpu.SemaphoreType.DMA((2,))]
        more = [d_hidden, gate, upward]
    elif first:
        out += [((tokens, rows), F32), (weight.shape, BF)]
        ins += [HBM]
        scratch = [pltpu.SemaphoreType.DMA((1,))]
        more = []
    else:
        out += [((tokens, rows), F32)]
        ins += [VMEM, VMEM]
        more = [d_hidden]
    return call(
        functools.partial(piece_kernel, steps, first, last),
        out,
        scratch,
        ins,
        outs,
        flops=4 * rows * tokens * columns,
        moved=4 * rows * columns,
    )(*own, *other, hidden, error, weight, *more)


def basis_slab(step, mine_ref, theirs_ref):
    chips = [back("x", hop, X) * Z + back("z", step, Z) for hop in range(X)]
    return jnp.concatenate([ref[chip] for chip in chips for ref in (mine_ref, theirs_ref)], axis=1)


def turn_kernel(layout, groups, *refs):
    n = len(layout)
    mine_ref, theirs_ref, out_ref, gram_ref = refs[n:]
    total, gram = 0.0, 0.0
    for matrix_ref, steps in zip(refs[:n], layout):
        basis = jnp.concatenate([basis_slab(step, mine_ref, theirs_ref) for step in steps], axis=1)
        total = total + lax.dot_general(matrix_ref[...].astype(BF), basis, NT, preferred_element_type=F32)
        gram = gram + lax.dot_general(basis, basis, NT, preferred_element_type=F32)
    gram_ref[...] = gram
    total = total.T
    for g in range(groups):
        out_ref[g] = total


def inverse_kernel(gram_ref, out_ref):
    n = gram_ref.shape[0]
    row = lax.broadcasted_iota(jnp.int32, (n, 2 * n), 0)
    col = lax.broadcasted_iota(jnp.int32, (n, 2 * n), 1)
    both = jnp.concatenate([gram_ref[...], jnp.zeros((n, n), F32)], axis=1) + jnp.where(col == row + n, 1.0, 0.0)
    for k in range(n):
        pivot = both[k:k + 1, k:k + 1]
        scaled = both[k:k + 1, :] * lax.rsqrt(pivot)
        column_k = both[:, k:k + 1] * lax.rsqrt(pivot)
        both = jnp.where(row > k, both - column_k * scaled, jnp.where(row == k, scaled, both))
    out_ref[...] = both[:, n:]


def final_kernel(layout, groups, *refs):
    n = len(layout)
    mine_ref, theirs_ref, terms_ref, inverse_ref, out_ref, q_ref, buf, sems = refs[n:]
    wide = mine_ref.shape[2]
    width = X * CORES * wide
    span = buf.shape[1] // X
    total = terms_ref[0]
    for g in range(1, groups):
        total = total + terms_ref[g]
    inverse = inverse_ref[...]
    next_q = jnp.dot(inverse, total / groups, precision=HIGHEST, preferred_element_type=F32)
    q_ref[...] = next_q
    factor = lax.dot_general(inverse, next_q, TN, precision=HIGHEST, preferred_element_type=F32)
    high, low = split(factor.T)
    factor = jnp.concatenate([high, low], axis=1)
    copies = []
    for hop in range(X):
        chip = back("x", hop, X)
        for matrix_ref, steps in zip(refs[:n], layout):
            for i, step in enumerate(steps):
                at = chip * Z + back("z", step, Z)
                basis = jnp.concatenate([mine_ref[at], theirs_ref[at]], axis=1)
                basis = jnp.concatenate([basis, basis], axis=0)
                start = i * width + hop * CORES * wide
                result = (matrix_ref[:, start:start + CORES * wide] - dot(factor, basis)).astype(BF)
                for c, place in enumerate(columns_of(step, hop, wide)):
                    buf[:, pl.ds(place, wide)] = result[:, c * wide:(c + 1) * wide]
        part = pl.ds(pl.multiple_of(chip * span, span), span)
        copies.append(fetch(buf.at[:, part], out_ref.at[:, part], sems.at[hop]))
    for copy in copies:
        copy.wait()


def local(gate, upward, cotangent, down_weight, error_buffer, start_q):
    groups = lax.axis_size("dp")
    rank = start_q.shape[1]
    tokens, wide = cotangent.shape
    error = error_buffer[0]
    rows, columns = error.shape
    tiles = tokens // LANES * rank

    blocks = [cotangent] + [shift(cotangent, "x", hop, X) for hop in range(1, X)]
    stacked, = call(stack_kernel, [((X, tokens, wide), BF)], ins=[None] + [VMEM] * (X - 1))(*blocks)
    pieces, others = {0: stacked}, {}

    hidden, send, mine, error = call(
        start_kernel,
        [((rows, tokens), BF), ((tiles + X * Z * rank, wide), BF), ((X * Z * rank, wide), BF), ((rows, columns), BF)],
        [
            pltpu.VMEM((rows, tokens), BF),
            pltpu.VMEM((rows, tokens), BF),
            pltpu.VMEM((rank, rows), F32),
            pltpu.SemaphoreType.DMA((X + 3,)),
        ],
        [HBM, HBM, HBM, HBM],
        flops=4 * rows * rank * columns,
        moved=2 * rows * columns,
    )(gate.T, upward.T, start_q.T, error)
    theirs = shift(send, "core", 1, CORES)
    terms, = call(pack_kernel, [((X, tiles + Z * rank, wide), BF)], ins=[VMEM] * 3)(send, theirs, mine)

    def ring(step):
        pieces[step] = shift(pieces[step - 1], "z", 1, Z)
        pieces[Z - step] = shift(pieces[(Z - step + 1) % Z], "z", Z - 1, Z)

    def swap(*steps):
        for step in steps:
            others[step] = shift(pieces[step], "core", 1, CORES)

    matrices, layout = [], []

    def use(steps, d_hidden, *more):
        matrix, *rest = add_pieces(steps, [pieces[s] for s in steps], [others[s] for s in steps], hidden, error, weight, d_hidden, *more)
        matrices.append(matrix)
        layout.append(steps)
        return rest if len(rest) > 1 else rest[0]

    weight = down_weight
    ring(1)
    swap(0)
    terms = exchange(terms, "x")
    terms, pieces[1], pieces[7] = lax.optimization_barrier((terms, pieces[1], pieces[7]))
    ring(2)
    swap(1, 7)
    terms, = call(repack_kernel, [((Z, tiles + rank, wide), BF)], ins=[VMEM])(terms)
    terms = exchange(terms, "z")
    d_hidden, weight = use((0,), None)
    terms, pieces[2], pieces[6], d_hidden = lax.optimization_barrier((terms, pieces[2], pieces[6], d_hidden))
    ring(3)
    swap(2, 6)
    terms, = call(functools.partial(slice_kernel, groups), [((groups, rank, wide), F32)], ins=[VMEM, None])(terms, cotangent)
    terms = exchange(terms, "dp")
    d_hidden = use((1, 7), d_hidden)
    terms, pieces[3], pieces[5], d_hidden = lax.optimization_barrier((terms, pieces[3], pieces[5], d_hidden))
    pieces[4] = shift(pieces[3], "z", 1, Z)
    swap(3, 5)
    mine, = call(spread_kernel, [((X * Z, rank, wide), BF)], ins=[VMEM])(terms)
    mine = exchange(mine, ("x", "z"))
    d_hidden = use((2, 6), d_hidden)
    swap(4)
    d_hidden = use((3, 5), d_hidden)
    mine, d_hidden = lax.optimization_barrier((mine, d_hidden))
    theirs = shift(mine, "core", 1, CORES)
    d_gate, d_up = use((4,), d_hidden, gate.T, upward.T)

    terms, gram = call(
        functools.partial(turn_kernel, tuple(layout), groups),
        [((groups, rank, rows), F32), ((rank, rank), F32)],
        ins=[VMEM] * (len(layout) + 2),
        flops=2 * rows * rank * columns,
        moved=4 * rows * columns,
    )(*matrices, mine, theirs)
    terms = exchange(terms, "dp")
    inverse, = call(inverse_kernel, [((rank, rank), F32)], ins=[VMEM])(gram)

    new_error, next_q = call(
        functools.partial(final_kernel, tuple(layout), groups),
        [((rows, columns), BF), ((rank, rows), F32)],
        [pltpu.VMEM((rows, columns), BF), pltpu.SemaphoreType.DMA((X,))],
        [VMEM] * (len(layout) + 4),
        [HBM, None],
        flops=4 * rows * rank * columns,
        moved=6 * rows * columns,
    )(*matrices, mine, theirs, terms, inverse)
    return (d_gate.T, d_up.T, new_error[None], next_q.T)


def solution(mesh):
    mesh = Mesh(mesh.devices.reshape(mesh.shape["dp"], X, Z, CORES), ("dp",) + PLANE)
    in_specs = (
        P("dp", PLANE),
        P("dp", PLANE),
        P("dp", PLANE),
        P(PLANE, None),
        P("dp", PLANE, None),
        P(PLANE, None),
    )
    out_specs = (P("dp", PLANE), P("dp", PLANE), P("dp", PLANE, None), P(PLANE, None))
    return jax.shard_map(local, mesh=mesh, in_specs=in_specs, out_specs=out_specs, check_vma=False)
```

```python
import functools

import jax
import jax.numpy as jnp
from jax import lax
from jax.experimental import pallas as pl
from jax.experimental.pallas import tpu as pltpu
from jax.sharding import Mesh, PartitionSpec as P

BF = jnp.bfloat16
F32 = jnp.float32
X, Z, CORES = 4, 8, 2
PLANE = ("x", "z", "core")
LANES = 128
NT = (((1,), (1,)), ((), ()))
TN = (((0,), (0,)), ((), ()))
VMEM = pl.BlockSpec(memory_space=pltpu.VMEM)
HBM = pl.BlockSpec(memory_space=pltpu.HBM)
HIGHEST = lax.Precision.HIGHEST


def dot(a, b):
    return jnp.dot(a, b, preferred_element_type=F32)


def split(a):
    high = a.astype(BF)
    return high, (a - high.astype(F32)).astype(BF)


def shift(a, axis, step, n):
    return lax.ppermute(a, axis, [(i, (i + step) % n) for i in range(n)])


def exchange(a, axis):
    return lax.all_to_all(a, axis, 0, 0)


def call(kernel, out, scratch=(), ins=None, outs=None, flops=0, moved=0, vmem=16):
    outs = outs if outs is not None else [VMEM] * len(out)
    run = pl.pallas_call(
        kernel,
        in_specs=[VMEM if spec is None else spec for spec in ins],
        out_specs=[VMEM if spec is None else spec for spec in outs],
        out_shape=[jax.ShapeDtypeStruct(s, t) if spec is None else spec.memory_space(s, t) for spec, (s, t) in zip(outs, out)],
        scratch_shapes=list(scratch),
        cost_estimate=pl.CostEstimate(flops=flops, bytes_accessed=moved, transcendentals=0),
        compiler_params=pltpu.CompilerParams(vmem_limit_bytes=vmem << 20),
    )

    def placed(a, spec):
        return a if spec is None else pltpu.with_memory_space_constraint(a, spec.memory_space)

    return lambda *args: run(*(placed(a, spec) for a, spec in zip(args, ins)))


def back(axis, step, n):
    return lax.rem(lax.axis_index(axis) + (n - step), n)


def columns_of(step, hop, wide):
    chip = back("x", hop, X) * Z + back("z", step, Z)
    core = lax.axis_index("core")
    return [pl.multiple_of((chip * CORES + c) * wide, wide) for c in (core, 1 - core)]


def slabs(ref, step, wide):
    return jnp.concatenate([ref[:, pl.ds(at, wide)] for hop in range(X) for at in columns_of(step, hop, wide)], axis=1)


def fetch(source, target, sem):
    copy = pltpu.make_async_copy(source, target, sem)
    copy.start()
    return copy


def start_kernel(gate_hbm, up_hbm, q_hbm, error_ref, hidden_ref, send_ref, mine_ref, error_buf, gate_ref, up_ref, q_ref, sems):
    rank = q_ref.shape[0]
    columns = error_ref.shape[1] // X
    small = [fetch(a, b, sems.at[X + i]) for i, (a, b) in enumerate(((gate_hbm, gate_ref), (up_hbm, up_ref), (q_hbm, q_ref)))]
    spans = [slice(x * columns, (x + 1) * columns) for x in range(X)]
    copies = [fetch(error_ref.at[:, spans[x]], error_buf.at[:, spans[x]], sems.at[x]) for x in range(X)]
    for copy in small:
        copy.wait()
    gate = gate_ref[...].astype(F32)
    hidden = (gate * jax.nn.sigmoid(gate) * up_ref[...].astype(F32)).astype(BF)
    hidden_ref[...] = hidden
    high, low = split(q_ref[...])
    both = jnp.concatenate([high, low], axis=0)
    left = dot(both, hidden)
    left = (left[:rank] + left[rank:]).astype(BF)
    blocks = left.shape[1] // LANES
    for b in range(blocks):
        send_ref[b * rank:(b + 1) * rank, :] = left[:, b * LANES:(b + 1) * LANES]
    first = lax.axis_index("core") == 0
    for x in range(X):
        copies[x].wait()
        term = dot(both, error_buf[:, spans[x]])
        term = (term[:rank] + term[rank:]).astype(BF)
        for z in range(Z):
            at = (x * Z + z) * rank
            zero = term[:, (2 * z) * LANES:(2 * z + 1) * LANES]
            one = term[:, (2 * z + 1) * LANES:(2 * z + 2) * LANES]
            mine_ref[at:at + rank, :] = jnp.where(first, zero, one)
            at += blocks * rank
            send_ref[at:at + rank, :] = jnp.where(first, one, zero)


def stack_kernel(*refs):
    for i, ref in enumerate(refs[:-1]):
        refs[-1][i] = ref[...]


def pack_kernel(send_ref, theirs_ref, mine_ref, out_ref):
    tiles = send_ref.shape[0] - mine_ref.shape[0]
    left = (send_ref[:tiles, :].astype(F32) + theirs_ref[:tiles, :].astype(F32)).astype(BF)
    part = (mine_ref[...].astype(F32) + theirs_ref[tiles:, :].astype(F32)).astype(BF)
    size = part.shape[0] // X
    for x in range(X):
        out_ref[x, :tiles, :] = left
        out_ref[x, tiles:, :] = part[x * size:(x + 1) * size]


def repack_kernel(terms_ref, out_ref):
    total = terms_ref[0].astype(F32)
    for x in range(1, X):
        total = total + terms_ref[x].astype(F32)
    total = total.astype(BF)
    rank = (terms_ref.shape[1] - out_ref.shape[1]) // (Z - 1)
    tiles = out_ref.shape[1] - rank
    for z in range(Z):
        out_ref[z, :tiles, :] = total[:tiles]
        out_ref[z, tiles:, :] = total[tiles + z * rank:tiles + (z + 1) * rank]


def slice_kernel(groups, terms_ref, cotangent_ref, out_ref):
    rank = out_ref.shape[0]
    terms = terms_ref[0].astype(F32)
    for i in range(1, Z):
        terms = terms + terms_ref[i].astype(F32)
    blocks = cotangent_ref.shape[0] // LANES
    total = terms[blocks * rank:]
    for b in range(blocks):
        total = total + dot(terms[b * rank:(b + 1) * rank].astype(BF), cotangent_ref[b * LANES:(b + 1) * LANES, :])
    out_ref[...] = total / groups


def ordered_sum(refs, buf):
    n = len(refs)
    for k, ref in enumerate(refs):
        buf[back("dp", k, n)] = ref[...]
    total = buf[0]
    for g in range(1, n):
        total = total + buf[g]
    return total


def spread_kernel(*refs):
    out_ref, buf = refs[-2:]
    total = ordered_sum(refs[:-2], buf).astype(BF)
    for i in range(out_ref.shape[0]):
        out_ref[i] = total


def piece_kernel(steps, first, last, *refs):
    n = len(steps)
    own, other = refs[:n], refs[n:2 * n]
    refs = refs[2 * n:]
    if first:
        hidden_ref, error_ref, weight_hbm, matrix_ref, d_ref, weight_ref, sem = refs
        copy = fetch(weight_hbm, weight_ref, sem.at[0])
    elif last:
        hidden_ref, error_ref, weight_ref, d_in, gate_hbm, up_hbm, matrix_ref, d_gate_ref, d_up_ref, gate_ref, up_ref, sem = refs
        pair = [fetch(gate_hbm, gate_ref, sem.at[0]), fetch(up_hbm, up_ref, sem.at[1])]
    else:
        hidden_ref, error_ref, weight_ref, d_in, matrix_ref, d_ref = refs
    wide = own[0].shape[2]
    blocks = [jnp.concatenate([ref[hop] for hop in range(X) for ref in (own[i], other[i])], axis=1) for i in range(n)]
    width = blocks[0].shape[1]
    for i, step in enumerate(steps):
        matrix_ref[:, i * width:(i + 1) * width] = slabs(error_ref, step, wide).astype(F32) + dot(hidden_ref[...], blocks[i])
    if first:
        copy.wait()
    block = jnp.concatenate(blocks, axis=1)
    weight = jnp.concatenate([slabs(weight_ref, step, wide) for step in steps], axis=1)
    total = lax.dot_general(block, weight, NT, preferred_element_type=F32)
    if not first:
        total = total + d_in[...]
    if not last:
        d_ref[...] = total
        return
    for copy in pair:
        copy.wait()
    total = total.T
    gate = gate_ref[...].astype(F32)
    sigma = jax.nn.sigmoid(gate)
    d_gate_ref[...] = (total * up_ref[...].astype(F32) * sigma * (1.0 + gate * (1.0 - sigma))).astype(BF)
    d_up_ref[...] = (total * (gate * sigma)).astype(BF)


def add_pieces(steps, own, other, hidden, error, weight, d_hidden, gate=None, upward=None):
    n = len(steps)
    tokens, wide = own[0].shape[1:]
    rows = hidden.shape[0]
    columns = n * X * CORES * wide
    first, last = d_hidden is None, gate is not None
    out = [((rows, columns), F32)]
    scratch, outs, ins = [], None, [VMEM] * (2 * n + 2)
    if last:
        out += [((rows, tokens), BF)] * 2
        outs = [VMEM, None, None]
        ins += [VMEM, VMEM, HBM, HBM]
        scratch = [pltpu.VMEM((rows, tokens), BF), pltpu.VMEM((rows, tokens), BF), pltpu.SemaphoreType.DMA((2,))]
        more = [d_hidden, gate, upward]
    elif first:
        out += [((tokens, rows), F32), (weight.shape, BF)]
        ins += [HBM]
        scratch = [pltpu.SemaphoreType.DMA((1,))]
        more = []
    else:
        out += [((tokens, rows), F32)]
        ins += [VMEM, VMEM]
        more = [d_hidden]
    return call(
        functools.partial(piece_kernel, steps, first, last),
        out,
        scratch,
        ins,
        outs,
        flops=4 * rows * tokens * columns,
        moved=4 * rows * columns,
    )(*own, *other, hidden, error, weight, *more)


def basis_slab(step, mine_ref, theirs_ref):
    chips = [back("x", hop, X) * Z + back("z", step, Z) for hop in range(X)]
    return jnp.concatenate([ref[chip] for chip in chips for ref in (mine_ref, theirs_ref)], axis=1)


def turn_kernel(layout, *refs):
    n = len(layout)
    mine_ref, theirs_ref, out_ref, gram_ref = refs[n:]
    total, gram = 0.0, 0.0
    for matrix_ref, steps in zip(refs[:n], layout):
        basis = jnp.concatenate([basis_slab(step, mine_ref, theirs_ref) for step in steps], axis=1)
        total = total + lax.dot_general(matrix_ref[...].astype(BF), basis, NT, preferred_element_type=F32)
        gram = gram + lax.dot_general(basis, basis, NT, preferred_element_type=F32)
    gram_ref[...] = gram
    out_ref[...] = total.T


def inverse_kernel(gram_ref, out_ref):
    n = gram_ref.shape[0]
    row = lax.broadcasted_iota(jnp.int32, (n, 2 * n), 0)
    col = lax.broadcasted_iota(jnp.int32, (n, 2 * n), 1)
    both = jnp.concatenate([gram_ref[...], jnp.zeros((n, n), F32)], axis=1) + jnp.where(col == row + n, 1.0, 0.0)
    for k in range(n):
        pivot = both[k:k + 1, k:k + 1]
        scaled = both[k:k + 1, :] * lax.rsqrt(pivot)
        column_k = both[:, k:k + 1] * lax.rsqrt(pivot)
        both = jnp.where(row > k, both - column_k * scaled, jnp.where(row == k, scaled, both))
    out_ref[...] = both[:, n:]


def final_kernel(layout, groups, *refs):
    n = len(layout)
    mine_ref, theirs_ref, inverse_ref = refs[n:n + 3]
    out_ref, q_ref, buf, terms_buf, sems = refs[n + 3 + groups:]
    wide = mine_ref.shape[2]
    width = X * CORES * wide
    span = buf.shape[1] // X
    total = ordered_sum(refs[n + 3:n + 3 + groups], terms_buf)
    inverse = inverse_ref[...]
    next_q = jnp.dot(inverse, total / groups, precision=HIGHEST, preferred_element_type=F32)
    q_ref[...] = next_q
    factor = lax.dot_general(inverse, next_q, TN, precision=HIGHEST, preferred_element_type=F32)
    high, low = split(factor.T)
    factor = jnp.concatenate([high, low], axis=1)
    copies = []
    for hop in range(X):
        chip = back("x", hop, X)
        for matrix_ref, steps in zip(refs[:n], layout):
            for i, step in enumerate(steps):
                at = chip * Z + back("z", step, Z)
                basis = jnp.concatenate([mine_ref[at], theirs_ref[at]], axis=1)
                basis = jnp.concatenate([basis, basis], axis=0)
                start = i * width + hop * CORES * wide
                result = (matrix_ref[:, start:start + CORES * wide] - dot(factor, basis)).astype(BF)
                for c, place in enumerate(columns_of(step, hop, wide)):
                    buf[:, pl.ds(place, wide)] = result[:, c * wide:(c + 1) * wide]
        part = pl.ds(pl.multiple_of(chip * span, span), span)
        copies.append(fetch(buf.at[:, part], out_ref.at[:, part], sems.at[hop]))
    for copy in copies:
        copy.wait()


def local(gate, upward, cotangent, down_weight, error_buffer, start_q):
    groups = lax.axis_size("dp")
    rank = start_q.shape[1]
    tokens, wide = cotangent.shape
    error = error_buffer[0]
    rows, columns = error.shape
    tiles = tokens // LANES * rank

    blocks = [cotangent] + [shift(cotangent, "x", hop, X) for hop in range(1, X)]
    stacked, = call(stack_kernel, [((X, tokens, wide), BF)], ins=[VMEM] * X)(*blocks)
    pieces, others = {0: stacked}, {}

    hidden, send, mine, error = call(
        start_kernel,
        [((rows, tokens), BF), ((tiles + X * Z * rank, wide), BF), ((X * Z * rank, wide), BF), ((rows, columns), BF)],
        [
            pltpu.VMEM((rows, tokens), BF),
            pltpu.VMEM((rows, tokens), BF),
            pltpu.VMEM((rank, rows), F32),
            pltpu.SemaphoreType.DMA((X + 3,)),
        ],
        [HBM, HBM, HBM, HBM],
        flops=4 * rows * rank * columns,
        moved=2 * rows * columns,
    )(gate.T, upward.T, start_q.T, error)
    theirs = shift(send, "core", 1, CORES)
    terms, = call(pack_kernel, [((X, tiles + Z * rank, wide), BF)], ins=[VMEM] * 3)(send, theirs, mine)

    def ring(step):
        pieces[step] = shift(pieces[step - 1], "z", 1, Z)
        pieces[Z - step] = shift(pieces[(Z - step + 1) % Z], "z", Z - 1, Z)

    def swap(*steps):
        for step in steps:
            others[step] = shift(pieces[step], "core", 1, CORES)

    matrices, layout = [], []

    def use(steps, d_hidden, *more):
        matrix, *rest = add_pieces(steps, [pieces[s] for s in steps], [others[s] for s in steps], hidden, error, weight, d_hidden, *more)
        matrices.append(matrix)
        layout.append(steps)
        return rest if len(rest) > 1 else rest[0]

    def around(a):
        return [a] + [shift(a, "dp", k, groups) for k in range(1, groups)]

    tie = lax.optimization_barrier
    weight = down_weight
    ring(1)
    swap(0)
    terms = exchange(terms, "x")
    terms, pieces[1], pieces[7] = tie((terms, pieces[1], pieces[7]))
    ring(2)
    swap(1, 7)
    terms, others[1], others[7] = tie((terms, others[1], others[7]))
    terms, = call(repack_kernel, [((Z, tiles + rank, wide), BF)], ins=[VMEM])(terms)
    terms = exchange(terms, "z")
    terms, pieces[2], pieces[6] = tie((terms, pieces[2], pieces[6]))
    ring(3)
    swap(2, 6)
    terms, = call(functools.partial(slice_kernel, groups), [((rank, wide), F32)], ins=[VMEM, VMEM])(terms, cotangent)
    terms = around(terms)
    d_hidden, weight = use((0, 1, 7), None)
    d_hidden = use((2, 6), d_hidden)
    mine, = call(spread_kernel, [((X * Z, rank, wide), BF)], [pltpu.VMEM((groups, rank, wide), F32)], [VMEM] * groups)(*terms)
    mine, pieces[3], pieces[5], d_hidden = tie((mine, pieces[3], pieces[5], d_hidden))
    pieces[4] = shift(pieces[3], "z", 1, Z)
    swap(3, 5)
    mine, others[3], others[5] = tie((mine, others[3], others[5]))
    mine = exchange(mine, ("x", "z"))
    mine, pieces[4], d_hidden = tie((mine, pieces[4], d_hidden))
    theirs = shift(mine, "core", 1, CORES)
    swap(4)
    d_hidden = use((3, 5), d_hidden)
    d_gate, d_up = use((4,), d_hidden, gate.T, upward.T)

    terms, gram = call(
        functools.partial(turn_kernel, tuple(layout)),
        [((rank, rows), F32), ((rank, rank), F32)],
        ins=[VMEM] * (len(layout) + 2),
        flops=2 * rows * rank * columns,
        moved=4 * rows * columns,
    )(*matrices, mine, theirs)
    terms = around(terms)
    inverse, = call(inverse_kernel, [((rank, rank), F32)], ins=[VMEM])(gram)

    new_error, next_q = call(
        functools.partial(final_kernel, tuple(layout), groups),
        [((rows, columns), BF), ((rank, rows), F32)],
        [pltpu.VMEM((rows, columns), BF), pltpu.VMEM((groups, rank, rows), F32), pltpu.SemaphoreType.DMA((X,))],
        [VMEM] * (len(layout) + 3 + groups),
        [HBM, None],
        flops=4 * rows * rank * columns,
        moved=6 * rows * columns,
    )(*matrices, mine, theirs, inverse, *terms)
    return (d_gate.T, d_up.T, new_error[None], next_q.T)


def solution(mesh):
    mesh = Mesh(mesh.devices.reshape(mesh.shape["dp"], X, Z, CORES), ("dp",) + PLANE)
    in_specs = (
        P("dp", PLANE),
        P("dp", PLANE),
        P("dp", PLANE),
        P(PLANE, None),
        P("dp", PLANE, None),
        P(PLANE, None),
    )
    out_specs = (P("dp", PLANE), P("dp", PLANE), P("dp", PLANE, None), P(PLANE, None))
    return jax.shard_map(local, mesh=mesh, in_specs=in_specs, out_specs=out_specs, check_vma=False)
```

```python
import functools

import jax
import jax.numpy as jnp
from jax import lax
from jax.experimental import pallas as pl
from jax.experimental.pallas import tpu as pltpu
from jax.sharding import Mesh, PartitionSpec as P

BF = jnp.bfloat16
F32 = jnp.float32
X, Z, CORES = 4, 8, 2
PLANE = ("x", "z", "core")
LANES = 128
NT = (((1,), (1,)), ((), ()))
TN = (((0,), (0,)), ((), ()))
VMEM = pl.BlockSpec(memory_space=pltpu.VMEM)
HBM = pl.BlockSpec(memory_space=pltpu.HBM)
HIGHEST = lax.Precision.HIGHEST


def dot(a, b):
    return jnp.dot(a, b, preferred_element_type=F32)


def split(a):
    high = a.astype(BF)
    return high, (a - high.astype(F32)).astype(BF)


def shift(a, axis, step, n):
    return lax.ppermute(a, axis, [(i, (i + step) % n) for i in range(n)])


def exchange(a, axis):
    return lax.all_to_all(a, axis, 0, 0)


def call(kernel, out, scratch=(), ins=None, outs=None, flops=0, moved=0, vmem=16):
    outs = outs if outs is not None else [VMEM] * len(out)
    run = pl.pallas_call(
        kernel,
        in_specs=[VMEM if spec is None else spec for spec in ins],
        out_specs=[VMEM if spec is None else spec for spec in outs],
        out_shape=[jax.ShapeDtypeStruct(s, t) if spec is None else spec.memory_space(s, t) for spec, (s, t) in zip(outs, out)],
        scratch_shapes=list(scratch),
        cost_estimate=pl.CostEstimate(flops=flops, bytes_accessed=moved, transcendentals=0),
        compiler_params=pltpu.CompilerParams(vmem_limit_bytes=vmem << 20),
    )

    def placed(a, spec):
        return a if spec is None else pltpu.with_memory_space_constraint(a, spec.memory_space)

    return lambda *args: run(*(placed(a, spec) for a, spec in zip(args, ins)))


def back(axis, step, n):
    return lax.rem(lax.axis_index(axis) + (n - step), n)


def chip_of(step, hop):
    return back("x", hop, X) * Z + back("z", step, Z)


def columns_of(step, hop, wide):
    core = lax.axis_index("core")
    return [pl.multiple_of((chip_of(step, hop) * CORES + c) * wide, wide) for c in (core, 1 - core)]


def fetch(source, target, sem):
    copy = pltpu.make_async_copy(source, target, sem)
    copy.start()
    return copy


def left_kernel(gate_hbm, up_hbm, q_hbm, hidden_hbm, left_ref, gate_ref, up_ref, q_ref, hidden_ref, sems):
    rank = q_ref.shape[0]
    for copy in [fetch(a, b, sems.at[i]) for i, (a, b) in enumerate(((gate_hbm, gate_ref), (up_hbm, up_ref), (q_hbm, q_ref)))]:
        copy.wait()
    gate = gate_ref[...].astype(F32)
    hidden = (gate * jax.nn.sigmoid(gate) * up_ref[...].astype(F32)).astype(BF)
    hidden_ref[...] = hidden
    copy = fetch(hidden_ref, hidden_hbm, sems.at[3])
    left = dot(jnp.concatenate(split(q_ref[...]), axis=0), hidden)
    left = (left[:rank] + left[rank:]).astype(BF)
    for b in range(left.shape[1] // LANES):
        left_ref[b * rank:(b + 1) * rank, :] = left[:, b * LANES:(b + 1) * LANES]
    copy.wait()


def chip_kernel(left_ref, theirs_ref, out_ref):
    left = (left_ref[...].astype(F32) + theirs_ref[...].astype(F32)).astype(BF)
    for z in range(Z):
        out_ref[z] = left


def error_kernel(q_hbm, error_ref, send_ref, mine_ref, q_ref, error_buf, sems):
    rank = q_ref.shape[0]
    columns = error_ref.shape[1] // X
    small = fetch(q_hbm, q_ref, sems.at[X])
    spans = [slice(x * columns, (x + 1) * columns) for x in range(X)]
    copies = [fetch(error_ref.at[:, spans[x]], error_buf.at[:, spans[x]], sems.at[x]) for x in range(X)]
    small.wait()
    both = jnp.concatenate(split(q_ref[...]), axis=0)
    first = lax.axis_index("core") == 0
    for x in range(X):
        copies[x].wait()
        term = dot(both, error_buf[:, spans[x]])
        term = (term[:rank] + term[rank:]).astype(BF)
        for z in range(Z):
            at = (x * Z + z) * rank
            zero = term[:, (2 * z) * LANES:(2 * z + 1) * LANES]
            one = term[:, (2 * z + 1) * LANES:(2 * z + 2) * LANES]
            mine_ref[at:at + rank, :] = jnp.where(first, zero, one)
            send_ref[at:at + rank, :] = jnp.where(first, one, zero)


def stack_kernel(*refs):
    for i, ref in enumerate(refs[:-1]):
        refs[-1][i] = ref[...]


def pack_kernel(left_ref, theirs_ref, mine_ref, out_ref):
    left = left_ref[0].astype(F32)
    for z in range(1, Z):
        left = left + left_ref[z].astype(F32)
    left = left.astype(BF)
    tiles = left.shape[0]
    part = (mine_ref[...].astype(F32) + theirs_ref[...].astype(F32)).astype(BF)
    size = part.shape[0] // X
    for x in range(X):
        out_ref[x, :tiles, :] = left
        out_ref[x, tiles:, :] = part[x * size:(x + 1) * size]


def repack_kernel(terms_ref, left_ref, part_ref):
    total = terms_ref[0].astype(F32)
    for x in range(1, X):
        total = total + terms_ref[x].astype(F32)
    total = total.astype(BF)
    tiles = left_ref.shape[0]
    rank = part_ref.shape[1]
    left_ref[...] = total[:tiles]
    for z in range(Z):
        part_ref[z] = total[tiles + z * rank:tiles + (z + 1) * rank]


def slice_kernel(groups, left_ref, part_ref, cotangent_ref, out_ref):
    rank = out_ref.shape[1]
    total = part_ref[0].astype(F32)
    for z in range(1, Z):
        total = total + part_ref[z].astype(F32)
    for b in range(cotangent_ref.shape[0] // LANES):
        total = total + dot(left_ref[b * rank:(b + 1) * rank, :], cotangent_ref[b * LANES:(b + 1) * LANES, :])
    total = total / groups
    for g in range(groups):
        out_ref[g] = total


def spread_kernel(terms_ref, out_ref):
    total = terms_ref[0]
    for g in range(1, terms_ref.shape[0]):
        total = total + terms_ref[g]
    total = total.astype(BF)
    for i in range(out_ref.shape[0]):
        out_ref[i] = total


def ordered_sum(refs, buf):
    n = len(refs)
    for k, ref in enumerate(refs):
        buf[back("dp", k, n)] = ref[...]
    total = buf[0]
    for g in range(1, n):
        total = total + buf[g]
    return total


def slab(ref, step, wide):
    return jnp.concatenate([ref[:, pl.ds(at, wide)] for hop in range(X) for at in columns_of(step, hop, wide)], axis=1)


def wait_all(copies):
    for copy in copies:
        copy.wait()


def piece_kernel(steps, *refs):
    n = len(steps)
    own, other = refs[:n], refs[n:2 * n]
    hidden_hbm, error_hbm, weight_hbm, gate_hbm, up_hbm, matrix_hbm, short_hbm, d_gate_ref, d_up_ref = refs[2 * n:2 * n + 9]
    own_buf, other_buf, hidden_ref, error_ref, weight_ref, gate_ref, up_ref, matrix_ref, short_ref, sems = refs[2 * n + 9:]
    wide = own_buf.shape[3]
    width = matrix_ref.shape[1] // n
    both = [fetch(hidden_hbm, hidden_ref, sems.at[0, n]), fetch(error_hbm, error_ref, sems.at[1, n])]
    copies = []
    for i in range(n):
        copies.append([fetch(own[i], own_buf.at[i], sems.at[0, i]), fetch(other[i], other_buf.at[i], sems.at[1, i])])
        if i == 0:
            late = [fetch(weight_hbm, weight_ref, sems.at[2, n])]
    pair = [fetch(gate_hbm, gate_ref, sems.at[0, n + 1]), fetch(up_hbm, up_ref, sems.at[1, n + 1])]
    wait_all(both)
    out = []
    total = None
    for i, step in enumerate(steps):
        wait_all(copies[i])
        block = jnp.concatenate([buf[i, hop] for hop in range(X) for buf in (own_buf, other_buf)], axis=1)
        span = pl.ds(i * width, width)
        matrix = slab(error_ref, step, wide).astype(F32) + dot(hidden_ref[...], block)
        matrix_ref[:, span] = matrix
        short_ref[:, span] = matrix.astype(BF)
        out.append(fetch(matrix_ref.at[:, span], matrix_hbm.at[:, span], sems.at[2, i]))
        out.append(fetch(short_ref.at[:, span], short_hbm.at[:, span], sems.at[3, i]))
        if i == 0:
            wait_all(late)
        term = lax.dot_general(block, slab(weight_ref, step, wide), NT, preferred_element_type=F32)
        total = term if total is None else total + term
    wait_all(pair)
    total = total.T
    gate = gate_ref[...].astype(F32)
    sigma = jax.nn.sigmoid(gate)
    d_gate_ref[...] = (total * up_ref[...].astype(F32) * sigma * (1.0 + gate * (1.0 - sigma))).astype(BF)
    d_up_ref[...] = (total * (gate * sigma)).astype(BF)
    wait_all(out)


def use_pieces(steps, own, other, hidden, error, weight, gate, upward):
    n = len(steps)
    tokens, wide = own[0].shape[1:]
    rows, columns = error.shape
    return call(
        functools.partial(piece_kernel, steps),
        [((rows, columns), F32), ((rows, columns), BF), ((rows, tokens), BF), ((rows, tokens), BF)],
        [
            pltpu.VMEM((n, X, tokens, wide), BF),
            pltpu.VMEM((n, X, tokens, wide), BF),
            pltpu.VMEM((rows, tokens), BF),
            pltpu.VMEM((rows, columns), BF),
            pltpu.VMEM((rows, columns), BF),
            pltpu.VMEM((rows, tokens), BF),
            pltpu.VMEM((rows, tokens), BF),
            pltpu.VMEM((rows, columns), F32),
            pltpu.VMEM((rows, columns), BF),
            pltpu.SemaphoreType.DMA((4, n + 2)),
        ],
        [HBM] * (2 * n + 5),
        [HBM, HBM, None, None],
        flops=4 * rows * tokens * columns,
        moved=30 << 20,
        vmem=52,
    )(*own, *other, hidden, error, weight, gate, upward)


def turn_kernel(steps, short_hbm, mine_ref, theirs_ref, out_ref, gram_ref, short_ref, sems):
    width = short_ref.shape[1] // len(steps)
    spans = [slice(i * width, (i + 1) * width) for i in range(len(steps))]
    copies = [fetch(short_hbm.at[:, span], short_ref.at[:, span], sems.at[i]) for i, span in enumerate(spans)]
    total, gram = 0.0, 0.0
    for i, step in enumerate(steps):
        basis = jnp.concatenate([ref[chip_of(step, hop)] for hop in range(X) for ref in (mine_ref, theirs_ref)], axis=1)
        gram = gram + lax.dot_general(basis, basis, NT, preferred_element_type=F32)
        copies[i].wait()
        total = total + lax.dot_general(short_ref[:, spans[i]], basis, NT, preferred_element_type=F32)
    gram_ref[...] = gram
    out_ref[...] = total.T


def inverse_kernel(gram_ref, out_ref):
    n = gram_ref.shape[0]
    row = lax.broadcasted_iota(jnp.int32, (n, 2 * n), 0)
    col = lax.broadcasted_iota(jnp.int32, (n, 2 * n), 1)
    both = jnp.concatenate([gram_ref[...], jnp.zeros((n, n), F32)], axis=1) + jnp.where(col == row + n, 1.0, 0.0)
    for k in range(n):
        pivot = both[k:k + 1, k:k + 1]
        scaled = both[k:k + 1, :] * lax.rsqrt(pivot)
        column_k = both[:, k:k + 1] * lax.rsqrt(pivot)
        both = jnp.where(row > k, both - column_k * scaled, jnp.where(row == k, scaled, both))
    out_ref[...] = both[:, n:]


def final_kernel(steps, groups, *refs):
    matrix_ref, mine_ref, theirs_ref, inverse_ref = refs[:4]
    out_ref, q_ref, buf, terms_buf, sems = refs[4 + groups:]
    wide = mine_ref.shape[2]
    width = CORES * wide
    span = buf.shape[1] // X
    total = ordered_sum(refs[4:4 + groups], terms_buf)
    inverse = inverse_ref[...]
    next_q = jnp.dot(inverse, total / groups, precision=HIGHEST, preferred_element_type=F32)
    q_ref[...] = next_q
    factor = lax.dot_general(inverse, next_q, TN, precision=HIGHEST, preferred_element_type=F32)
    high, low = split(factor.T)
    factor = jnp.concatenate([high, low], axis=1)
    copies = []
    for hop in range(X):
        for i, step in enumerate(steps):
            at = chip_of(step, hop)
            basis = jnp.concatenate([mine_ref[at], theirs_ref[at]], axis=1)
            basis = jnp.concatenate([basis, basis], axis=0)
            start = (i * X + hop) * width
            result = (matrix_ref[:, start:start + width] - dot(factor, basis)).astype(BF)
            for c, place in enumerate(columns_of(step, hop, wide)):
                buf[:, pl.ds(place, wide)] = result[:, c * wide:(c + 1) * wide]
        part = pl.ds(pl.multiple_of(back("x", hop, X) * span, span), span)
        copies.append(fetch(buf.at[:, part], out_ref.at[:, part], sems.at[hop]))
    wait_all(copies)


def local(gate, upward, cotangent, down_weight, error_buffer, start_q):
    groups = lax.axis_size("dp")
    rank = start_q.shape[1]
    tokens, wide = cotangent.shape
    error = error_buffer[0]
    rows, columns = error.shape
    tiles = tokens // LANES * rank
    tie = lax.optimization_barrier

    blocks = [cotangent] + [shift(cotangent, "x", hop, X) for hop in range(1, X)]
    hidden, left = call(
        left_kernel,
        [((rows, tokens), BF), ((tiles, LANES), BF)],
        [
            pltpu.VMEM((rows, tokens), BF),
            pltpu.VMEM((rows, tokens), BF),
            pltpu.VMEM((rank, rows), F32),
            pltpu.VMEM((rows, tokens), BF),
            pltpu.SemaphoreType.DMA((4,)),
        ],
        [HBM] * 3,
        [HBM, VMEM],
        moved=6 * rows * tokens,
    )(gate.T, upward.T, start_q.T)
    theirs = shift(left, "core", 1, CORES)
    send, mine = call(
        error_kernel,
        [((X * Z * rank, wide), BF), ((X * Z * rank, wide), BF)],
        [pltpu.VMEM((rank, rows), F32), pltpu.VMEM((rows, columns), BF), pltpu.SemaphoreType.DMA((X + 1,))],
        [HBM, HBM],
        flops=4 * rows * rank * columns,
        moved=2 * rows * columns,
    )(start_q.T, error)
    part = shift(send, "core", 1, CORES)
    tied = tie((left, theirs, *blocks[1:]))
    left, theirs, blocks[1:] = tied[0], tied[1], tied[2:]
    stacked, = call(stack_kernel, [((X, tokens, wide), BF)], ins=[None] * X, outs=[None])(*blocks)
    pieces, others = {0: stacked}, {}
    steps = (0, 1, 7, 2, 6, 3, 5, 4)

    def ring(step, payload=None):
        up, down = pieces[step - 1], pieces[(Z - step + 1) % Z]
        if payload is not None:
            payload, up, down = tie((payload, up, down))
        pieces[step] = shift(up, "z", 1, Z)
        if step < Z // 2:
            pieces[Z - step] = shift(down, "z", Z - 1, Z)
        return payload

    def swap(*steps):
        for step in steps:
            others[step] = shift(pieces[step], "core", 1, CORES)

    left, = call(chip_kernel, [((Z, tiles, LANES), BF)], ins=[VMEM, VMEM])(left, theirs)
    left = ring(1, left)
    swap(0)
    left = exchange(left, "z")
    left, pieces[1], pieces[7] = tie((left, pieces[1], pieces[7]))
    terms, = call(pack_kernel, [((X, tiles + Z * rank, wide), BF)], ins=[VMEM] * 3)(left, part, mine)
    terms = ring(2, terms)
    swap(1, 7)
    terms = exchange(terms, "x")
    terms, pieces[2], pieces[6] = tie((terms, pieces[2], pieces[6]))
    left, part = call(repack_kernel, [((tiles, LANES), BF), ((Z, rank, wide), BF)], ins=[VMEM])(terms)
    part = ring(3, part)
    swap(2, 6)
    part = exchange(part, "z")
    part, pieces[3], pieces[5] = tie((part, pieces[3], pieces[5]))
    terms, = call(functools.partial(slice_kernel, groups), [((groups, rank, wide), F32)], ins=[VMEM, VMEM, None])(left, part, cotangent)
    terms = ring(4, terms)
    swap(3, 5)
    terms = exchange(terms, "dp")
    terms, pieces[4] = tie((terms, pieces[4]))
    mine, = call(spread_kernel, [((X * Z, rank, wide), BF)], ins=[VMEM])(terms)
    mine = exchange(mine, ("x", "z"))
    swap(4)
    matrix, short, d_gate, d_up = use_pieces(
        steps, [pieces[s] for s in steps], [others[s] for s in steps], hidden, error, down_weight, gate.T, upward.T)
    mine, short = tie((mine, short))
    theirs = shift(mine, "core", 1, CORES)

    terms, gram = call(
        functools.partial(turn_kernel, steps),
        [((rank, rows), F32), ((rank, rank), F32)],
        [pltpu.VMEM((rows, columns), BF), pltpu.SemaphoreType.DMA((Z,))],
        [HBM, VMEM, VMEM],
        flops=2 * rows * rank * columns,
        moved=4 * rows * columns,
    )(short, mine, theirs)
    terms = [terms] + [shift(terms, "dp", k, groups) for k in range(1, groups)]
    inverse, = call(inverse_kernel, [((rank, rank), F32)], ins=[VMEM])(gram)

    new_error, next_q = call(
        functools.partial(final_kernel, steps, groups),
        [((rows, columns), BF), ((rank, rows), F32)],
        [pltpu.VMEM((rows, columns), BF), pltpu.VMEM((groups, rank, rows), F32), pltpu.SemaphoreType.DMA((X,))],
        [VMEM] * (4 + groups),
        [HBM, None],
        flops=4 * rows * rank * columns,
        moved=6 * rows * columns,
    )(matrix, mine, theirs, inverse, *terms)
    return (d_gate.T, d_up.T, new_error[None], next_q.T)


def solution(mesh):
    mesh = Mesh(mesh.devices.reshape(mesh.shape["dp"], X, Z, CORES), ("dp",) + PLANE)
    in_specs = (
        P("dp", PLANE),
        P("dp", PLANE),
        P("dp", PLANE),
        P(PLANE, None),
        P("dp", PLANE, None),
        P(PLANE, None),
    )
    out_specs = (P("dp", PLANE), P("dp", PLANE), P("dp", PLANE, None), P(PLANE, None))
    return jax.shard_map(local, mesh=mesh, in_specs=in_specs, out_specs=out_specs, check_vma=False)
```

```python
import functools

import jax
import jax.numpy as jnp
from jax import lax
from jax.experimental import pallas as pl
from jax.experimental.pallas import tpu as pltpu
from jax.sharding import Mesh, PartitionSpec as P

BF = jnp.bfloat16
F32 = jnp.float32
X, Z, CORES = 4, 8, 2
PLANE = ("x", "z", "core")
LANES = 128
NT = (((1,), (1,)), ((), ()))
TN = (((0,), (0,)), ((), ()))
VMEM = pl.BlockSpec(memory_space=pltpu.VMEM)
HBM = pl.BlockSpec(memory_space=pltpu.HBM)
HIGHEST = lax.Precision.HIGHEST


def dot(a, b):
    return jnp.dot(a, b, preferred_element_type=F32)


def split(a):
    high = a.astype(BF)
    return high, (a - high.astype(F32)).astype(BF)


def shift(a, axis, step, n):
    return lax.ppermute(a, axis, [(i, (i + step) % n) for i in range(n)])


def exchange(a, axis):
    return lax.all_to_all(a, axis, 0, 0)


def call(kernel, out, scratch=(), ins=None, outs=None, flops=0, moved=0, vmem=16):
    outs = outs if outs is not None else [VMEM] * len(out)
    run = pl.pallas_call(
        kernel,
        in_specs=[VMEM if spec is None else spec for spec in ins],
        out_specs=[VMEM if spec is None else spec for spec in outs],
        out_shape=[jax.ShapeDtypeStruct(s, t) if spec is None else spec.memory_space(s, t) for spec, (s, t) in zip(outs, out)],
        scratch_shapes=list(scratch),
        cost_estimate=pl.CostEstimate(flops=flops, bytes_accessed=moved, transcendentals=0),
        compiler_params=pltpu.CompilerParams(vmem_limit_bytes=vmem << 20),
    )

    def placed(a, spec):
        return a if spec is None else pltpu.with_memory_space_constraint(a, spec.memory_space)

    return lambda *args: run(*(placed(a, spec) for a, spec in zip(args, ins)))


def back(axis, step, n):
    return lax.rem(lax.axis_index(axis) + (n - step), n)


def chip_of(step, hop):
    return back("x", hop, X) * Z + back("z", step, Z)


def columns_of(step, hop, wide):
    core = lax.axis_index("core")
    return [pl.multiple_of((chip_of(step, hop) * CORES + c) * wide, wide) for c in (core, 1 - core)]


def fetch(source, target, sem):
    copy = pltpu.make_async_copy(source, target, sem)
    copy.start()
    return copy


def left_kernel(gate_hbm, up_hbm, q_hbm, hidden_hbm, left_ref, gate_ref, up_ref, q_ref, hidden_ref, sems):
    rank = q_ref.shape[0]
    for copy in [fetch(a, b, sems.at[i]) for i, (a, b) in enumerate(((gate_hbm, gate_ref), (up_hbm, up_ref), (q_hbm, q_ref)))]:
        copy.wait()
    gate = gate_ref[...].astype(F32)
    hidden = (gate * jax.nn.sigmoid(gate) * up_ref[...].astype(F32)).astype(BF)
    hidden_ref[...] = hidden
    copy = fetch(hidden_ref, hidden_hbm, sems.at[3])
    left = dot(jnp.concatenate(split(q_ref[...]), axis=0), hidden)
    left = (left[:rank] + left[rank:]).astype(BF)
    for b in range(left.shape[1] // LANES):
        left_ref[b * rank:(b + 1) * rank, :] = left[:, b * LANES:(b + 1) * LANES]
    copy.wait()


def chip_kernel(left_ref, theirs_ref, out_ref):
    left = (left_ref[...].astype(F32) + theirs_ref[...].astype(F32)).astype(BF)
    for z in range(Z):
        out_ref[z] = left


def error_kernel(q_hbm, error_ref, send_ref, mine_ref, q_ref, error_buf, sems):
    rank = q_ref.shape[0]
    columns = error_ref.shape[1] // X
    small = fetch(q_hbm, q_ref, sems.at[X])
    spans = [slice(x * columns, (x + 1) * columns) for x in range(X)]
    copies = [fetch(error_ref.at[:, spans[x]], error_buf.at[:, spans[x]], sems.at[x]) for x in range(X)]
    small.wait()
    both = jnp.concatenate(split(q_ref[...]), axis=0)
    first = lax.axis_index("core") == 0
    for x in range(X):
        copies[x].wait()
        term = dot(both, error_buf[:, spans[x]])
        term = (term[:rank] + term[rank:]).astype(BF)
        for z in range(Z):
            at = (x * Z + z) * rank
            zero = term[:, (2 * z) * LANES:(2 * z + 1) * LANES]
            one = term[:, (2 * z + 1) * LANES:(2 * z + 2) * LANES]
            mine_ref[at:at + rank, :] = jnp.where(first, zero, one)
            send_ref[at:at + rank, :] = jnp.where(first, one, zero)


def stack_kernel(*refs):
    for i, ref in enumerate(refs[:-1]):
        refs[-1][i] = ref[...]


def pack_kernel(left_ref, theirs_ref, mine_ref, out_ref):
    left = left_ref[0].astype(F32)
    for z in range(1, Z):
        left = left + left_ref[z].astype(F32)
    left = left.astype(BF)
    tiles = left.shape[0]
    part = (mine_ref[...].astype(F32) + theirs_ref[...].astype(F32)).astype(BF)
    size = part.shape[0] // X
    for x in range(X):
        out_ref[x, :tiles, :] = left
        out_ref[x, tiles:, :] = part[x * size:(x + 1) * size]


def repack_kernel(terms_ref, left_ref, part_ref):
    total = terms_ref[0].astype(F32)
    for x in range(1, X):
        total = total + terms_ref[x].astype(F32)
    total = total.astype(BF)
    tiles = left_ref.shape[0]
    rank = part_ref.shape[1]
    left_ref[...] = total[:tiles]
    for z in range(Z):
        part_ref[z] = total[tiles + z * rank:tiles + (z + 1) * rank]


def slice_kernel(groups, left_ref, part_ref, cotangent_ref, out_ref):
    rank = out_ref.shape[1]
    total = part_ref[0].astype(F32)
    for z in range(1, Z):
        total = total + part_ref[z].astype(F32)
    for b in range(cotangent_ref.shape[0] // LANES):
        total = total + dot(left_ref[b * rank:(b + 1) * rank, :], cotangent_ref[b * LANES:(b + 1) * LANES, :])
    total = total / groups
    for g in range(groups):
        out_ref[g] = total


def spread_kernel(terms_ref, out_ref):
    total = terms_ref[0]
    for g in range(1, terms_ref.shape[0]):
        total = total + terms_ref[g]
    total = total.astype(BF)
    for i in range(out_ref.shape[0]):
        out_ref[i] = total


def ordered_sum(refs, buf):
    n = len(refs)
    for k, ref in enumerate(refs):
        buf[back("dp", k, n)] = ref[...]
    total = buf[0]
    for g in range(1, n):
        total = total + buf[g]
    return total


def slab(ref, step, wide):
    return jnp.concatenate([ref[:, pl.ds(at, wide)] for hop in range(X) for at in columns_of(step, hop, wide)], axis=1)


def wait_all(copies):
    for copy in copies:
        copy.wait()


def piece_kernel(steps, *refs):
    n = len(steps)
    own, other = refs[:n], refs[n:2 * n]
    hidden_hbm, error_hbm, weight_hbm, gate_hbm, up_hbm, matrix_hbm, d_gate_ref, d_up_ref = refs[2 * n:2 * n + 8]
    own_buf, other_buf, hidden_ref, error_ref, weight_ref, gate_ref, up_ref, matrix_ref, sems = refs[2 * n + 8:]
    wide = own_buf.shape[3]
    width = matrix_ref.shape[1] // n
    both = [fetch(hidden_hbm, hidden_ref, sems.at[0, n]), fetch(error_hbm, error_ref, sems.at[1, n])]
    copies = []
    for i in range(n):
        copies.append([fetch(own[i], own_buf.at[i], sems.at[0, i]), fetch(other[i], other_buf.at[i], sems.at[1, i])])
        if i == 0:
            late = [fetch(weight_hbm, weight_ref, sems.at[2, n])]
    pair = [fetch(gate_hbm, gate_ref, sems.at[0, n + 1]), fetch(up_hbm, up_ref, sems.at[1, n + 1])]
    wait_all(both)
    out = []
    total = None
    for i, step in enumerate(steps):
        wait_all(copies[i])
        block = jnp.concatenate([buf[i, hop] for hop in range(X) for buf in (own_buf, other_buf)], axis=1)
        span = pl.ds(i * width, width)
        matrix_ref[:, span] = slab(error_ref, step, wide).astype(F32) + dot(hidden_ref[...], block)
        out.append(fetch(matrix_ref.at[:, span], matrix_hbm.at[:, span], sems.at[2, i]))
        if i == 0:
            wait_all(late)
        term = lax.dot_general(block, slab(weight_ref, step, wide), NT, preferred_element_type=F32)
        total = term if total is None else total + term
    wait_all(pair)
    total = total.T
    gate = gate_ref[...].astype(F32)
    sigma = jax.nn.sigmoid(gate)
    d_gate_ref[...] = (total * up_ref[...].astype(F32) * sigma * (1.0 + gate * (1.0 - sigma))).astype(BF)
    d_up_ref[...] = (total * (gate * sigma)).astype(BF)
    wait_all(out)


def use_pieces(steps, own, other, hidden, error, weight, gate, upward):
    n = len(steps)
    tokens, wide = own[0].shape[1:]
    rows, columns = error.shape
    return call(
        functools.partial(piece_kernel, steps),
        [((rows, columns), F32), ((rows, tokens), BF), ((rows, tokens), BF)],
        [
            pltpu.VMEM((n, X, tokens, wide), BF),
            pltpu.VMEM((n, X, tokens, wide), BF),
            pltpu.VMEM((rows, tokens), BF),
            pltpu.VMEM((rows, columns), BF),
            pltpu.VMEM((rows, columns), BF),
            pltpu.VMEM((rows, tokens), BF),
            pltpu.VMEM((rows, tokens), BF),
            pltpu.VMEM((rows, columns), F32),
            pltpu.SemaphoreType.DMA((3, n + 2)),
        ],
        [HBM] * (2 * n + 5),
        [HBM, None, None],
        flops=4 * rows * tokens * columns,
        moved=30 << 20,
        vmem=52,
    )(*own, *other, hidden, error, weight, gate, upward)


def load_kernel(source_hbm, out_ref, sems):
    part = source_hbm.shape[1] // X
    spans = [pl.ds(i * part, part) for i in range(X)]
    wait_all([fetch(source_hbm.at[:, span], out_ref.at[:, span], sems.at[i]) for i, span in enumerate(spans)])


def turn_kernel(steps, matrix_ref, mine_ref, theirs_ref, out_ref, gram_ref):
    chips = [chip_of(step, hop) for step in steps for hop in range(X)]
    basis = jnp.concatenate([ref[chip] for chip in chips for ref in (mine_ref, theirs_ref)], axis=1)
    gram_ref[...] = lax.dot_general(basis, basis, NT, preferred_element_type=F32)
    out_ref[...] = lax.dot_general(matrix_ref[...].astype(BF), basis, NT, preferred_element_type=F32).T


def inverse_kernel(gram_ref, out_ref):
    n = gram_ref.shape[0]
    row = lax.broadcasted_iota(jnp.int32, (n, 2 * n), 0)
    col = lax.broadcasted_iota(jnp.int32, (n, 2 * n), 1)
    both = jnp.concatenate([gram_ref[...], jnp.zeros((n, n), F32)], axis=1) + jnp.where(col == row + n, 1.0, 0.0)
    for k in range(n):
        pivot = both[k:k + 1, k:k + 1]
        scaled = both[k:k + 1, :] * lax.rsqrt(pivot)
        column_k = both[:, k:k + 1] * lax.rsqrt(pivot)
        both = jnp.where(row > k, both - column_k * scaled, jnp.where(row == k, scaled, both))
    out_ref[...] = both[:, n:]


def final_kernel(steps, groups, *refs):
    matrix_ref, mine_ref, theirs_ref, inverse_ref = refs[:4]
    out_ref, q_ref, buf, terms_buf, sems = refs[4 + groups:]
    wide = mine_ref.shape[2]
    width = CORES * wide
    span = buf.shape[1] // X
    total = ordered_sum(refs[4:4 + groups], terms_buf)
    inverse = inverse_ref[...]
    next_q = jnp.dot(inverse, total / groups, precision=HIGHEST, preferred_element_type=F32)
    q_ref[...] = next_q
    factor = lax.dot_general(inverse, next_q, TN, precision=HIGHEST, preferred_element_type=F32)
    high, low = split(factor.T)
    factor = jnp.concatenate([high, low], axis=1)
    copies = []
    for hop in range(X):
        for i, step in enumerate(steps):
            at = chip_of(step, hop)
            basis = jnp.concatenate([mine_ref[at], theirs_ref[at]], axis=1)
            basis = jnp.concatenate([basis, basis], axis=0)
            start = (i * X + hop) * width
            result = (matrix_ref[:, start:start + width] - dot(factor, basis)).astype(BF)
            for c, place in enumerate(columns_of(step, hop, wide)):
                buf[:, pl.ds(place, wide)] = result[:, c * wide:(c + 1) * wide]
        part = pl.ds(pl.multiple_of(back("x", hop, X) * span, span), span)
        copies.append(fetch(buf.at[:, part], out_ref.at[:, part], sems.at[hop]))
    wait_all(copies)


def local(gate, upward, cotangent, down_weight, error_buffer, start_q):
    groups = lax.axis_size("dp")
    rank = start_q.shape[1]
    tokens, wide = cotangent.shape
    error = error_buffer[0]
    rows, columns = error.shape
    tiles = tokens // LANES * rank
    tie = lax.optimization_barrier

    blocks = [cotangent] + [shift(cotangent, "x", hop, X) for hop in range(1, X)]
    hidden, left = call(
        left_kernel,
        [((rows, tokens), BF), ((tiles, LANES), BF)],
        [
            pltpu.VMEM((rows, tokens), BF),
            pltpu.VMEM((rows, tokens), BF),
            pltpu.VMEM((rank, rows), F32),
            pltpu.VMEM((rows, tokens), BF),
            pltpu.SemaphoreType.DMA((4,)),
        ],
        [HBM] * 3,
        [HBM, VMEM],
        moved=6 * rows * tokens,
    )(gate.T, upward.T, start_q.T)
    theirs = shift(left, "core", 1, CORES)
    send, mine = call(
        error_kernel,
        [((X * Z * rank, wide), BF), ((X * Z * rank, wide), BF)],
        [pltpu.VMEM((rank, rows), F32), pltpu.VMEM((rows, columns), BF), pltpu.SemaphoreType.DMA((X + 1,))],
        [HBM, HBM],
        flops=4 * rows * rank * columns,
        moved=2 * rows * columns,
    )(start_q.T, error)
    part = shift(send, "core", 1, CORES)
    tied = tie((left, theirs, *blocks[1:]))
    left, theirs, blocks[1:] = tied[0], tied[1], tied[2:]
    stacked, = call(stack_kernel, [((X, tokens, wide), BF)], ins=[None] * X, outs=[None])(*blocks)
    pieces, others = {0: stacked}, {}
    steps = (0, 1, 7, 2, 6, 3, 5, 4)

    def ring(step, payload=None):
        up, down = pieces[step - 1], pieces[(Z - step + 1) % Z]
        pieces[step] = shift(up, "z", 1, Z)
        if step < Z // 2:
            pieces[Z - step] = shift(down, "z", Z - 1, Z)
        return payload

    def swap(*steps):
        for step in steps:
            others[step] = shift(pieces[step], "core", 1, CORES)

    left, = call(chip_kernel, [((Z, tiles, LANES), BF)], ins=[VMEM, VMEM])(left, theirs)
    left = ring(1, left)
    swap(0)
    left = exchange(left, "z")
    left, pieces[1], pieces[7] = tie((left, pieces[1], pieces[7]))
    terms, = call(pack_kernel, [((X, tiles + Z * rank, wide), BF)], ins=[VMEM] * 3)(left, part, mine)
    terms = ring(2, terms)
    swap(1, 7)
    terms = exchange(terms, "x")
    terms, pieces[2], pieces[6] = tie((terms, pieces[2], pieces[6]))
    left, part = call(repack_kernel, [((tiles, LANES), BF), ((Z, rank, wide), BF)], ins=[VMEM])(terms)
    part = ring(3, part)
    swap(2, 6)
    part = exchange(part, "z")
    part, pieces[3], pieces[5] = tie((part, pieces[3], pieces[5]))
    terms, = call(functools.partial(slice_kernel, groups), [((groups, rank, wide), F32)], ins=[VMEM, VMEM, None])(left, part, cotangent)
    terms = ring(4, terms)
    swap(3, 5)
    terms = exchange(terms, "dp")
    terms, pieces[4] = tie((terms, pieces[4]))
    mine, = call(spread_kernel, [((X * Z, rank, wide), BF)], ins=[VMEM])(terms)
    mine = exchange(mine, ("x", "z"))
    swap(4)
    matrix, d_gate, d_up = use_pieces(
        steps, [pieces[s] for s in steps], [others[s] for s in steps], hidden, error, down_weight, gate.T, upward.T)
    mine, matrix = tie((mine, matrix))
    theirs = shift(mine, "core", 1, CORES)
    matrix, = call(load_kernel, [((rows, columns), F32)], [pltpu.SemaphoreType.DMA((X,))], [HBM])(matrix)

    terms, gram = call(
        functools.partial(turn_kernel, steps),
        [((rank, rows), F32), ((rank, rank), F32)],
        ins=[VMEM] * 3,
        flops=2 * rows * rank * columns,
        moved=4 * rows * columns,
    )(matrix, mine, theirs)
    terms = [terms] + [shift(terms, "dp", k, groups) for k in range(1, groups)]
    inverse, = call(inverse_kernel, [((rank, rank), F32)], ins=[VMEM])(gram)

    new_error, next_q = call(
        functools.partial(final_kernel, steps, groups),
        [((rows, columns), BF), ((rank, rows), F32)],
        [pltpu.VMEM((rows, columns), BF), pltpu.VMEM((groups, rank, rows), F32), pltpu.SemaphoreType.DMA((X,))],
        [VMEM] * (4 + groups),
        [HBM, None],
        flops=4 * rows * rank * columns,
        moved=6 * rows * columns,
    )(matrix, mine, theirs, inverse, *terms)
    return (d_gate.T, d_up.T, new_error[None], next_q.T)


def solution(mesh):
    mesh = Mesh(mesh.devices.reshape(mesh.shape["dp"], X, Z, CORES), ("dp",) + PLANE)
    in_specs = (
        P("dp", PLANE),
        P("dp", PLANE),
        P("dp", PLANE),
        P(PLANE, None),
        P("dp", PLANE, None),
        P(PLANE, None),
    )
    out_specs = (P("dp", PLANE), P("dp", PLANE), P("dp", PLANE, None), P(PLANE, None))
    return jax.shard_map(local, mesh=mesh, in_specs=in_specs, out_specs=out_specs, check_vma=False)
```

```python
import functools

import jax
import jax.numpy as jnp
from jax import lax
from jax.experimental import pallas as pl
from jax.experimental.pallas import tpu as pltpu
from jax.sharding import Mesh, PartitionSpec as P

BF = jnp.bfloat16
F32 = jnp.float32
X, Z, CORES = 4, 8, 2
PLANE = ("x", "z", "core")
LANES = 128
NT = (((1,), (1,)), ((), ()))
TN = (((0,), (0,)), ((), ()))
VMEM = pl.BlockSpec(memory_space=pltpu.VMEM)
HBM = pl.BlockSpec(memory_space=pltpu.HBM)
HIGHEST = lax.Precision.HIGHEST


def dot(a, b):
    return jnp.dot(a, b, preferred_element_type=F32)


def split(a):
    high = a.astype(BF)
    return high, (a - high.astype(F32)).astype(BF)


def shift(a, axis, step, n):
    return lax.ppermute(a, axis, [(i, (i + step) % n) for i in range(n)])


def exchange(a, axis):
    return lax.all_to_all(a, axis, 0, 0)


def call(kernel, out, scratch=(), ins=None, outs=None, flops=0, moved=0, vmem=16):
    outs = outs if outs is not None else [VMEM] * len(out)
    run = pl.pallas_call(
        kernel,
        in_specs=[VMEM if spec is None else spec for spec in ins],
        out_specs=[VMEM if spec is None else spec for spec in outs],
        out_shape=[jax.ShapeDtypeStruct(s, t) if spec is None else spec.memory_space(s, t) for spec, (s, t) in zip(outs, out)],
        scratch_shapes=list(scratch),
        cost_estimate=pl.CostEstimate(flops=flops, bytes_accessed=moved, transcendentals=0),
        compiler_params=pltpu.CompilerParams(vmem_limit_bytes=vmem << 20),
    )

    def placed(a, spec):
        return a if spec is None else pltpu.with_memory_space_constraint(a, spec.memory_space)

    return lambda *args: run(*(placed(a, spec) for a, spec in zip(args, ins)))


def back(axis, step, n):
    return lax.rem(lax.axis_index(axis) + (n - step), n)


def chip_of(step, hop):
    return back("x", hop, X) * Z + back("z", step, Z)


def columns_of(step, hop, wide):
    core = lax.axis_index("core")
    return [pl.multiple_of((chip_of(step, hop) * CORES + c) * wide, wide) for c in (core, 1 - core)]


def fetch(source, target, sem):
    copy = pltpu.make_async_copy(source, target, sem)
    copy.start()
    return copy


def left_kernel(gate_hbm, up_hbm, q_hbm, hidden_hbm, left_ref, gate_ref, up_ref, q_ref, hidden_ref, sems):
    rank = q_ref.shape[0]
    for copy in [fetch(a, b, sems.at[i]) for i, (a, b) in enumerate(((gate_hbm, gate_ref), (up_hbm, up_ref), (q_hbm, q_ref)))]:
        copy.wait()
    gate = gate_ref[...].astype(F32)
    hidden = (gate * jax.nn.sigmoid(gate) * up_ref[...].astype(F32)).astype(BF)
    hidden_ref[...] = hidden
    copy = fetch(hidden_ref, hidden_hbm, sems.at[3])
    left = dot(jnp.concatenate(split(q_ref[...]), axis=0), hidden)
    left = (left[:rank] + left[rank:]).astype(BF)
    for b in range(left.shape[1] // LANES):
        left_ref[b * rank:(b + 1) * rank, :] = left[:, b * LANES:(b + 1) * LANES]
    copy.wait()


def chip_kernel(left_ref, theirs_ref, out_ref):
    left = (left_ref[...].astype(F32) + theirs_ref[...].astype(F32)).astype(BF)
    for z in range(Z):
        out_ref[z] = left


def error_kernel(q_hbm, error_ref, send_ref, mine_ref, q_ref, error_buf, sems):
    rank = q_ref.shape[0]
    columns = error_ref.shape[1] // X
    small = fetch(q_hbm, q_ref, sems.at[X])
    spans = [slice(x * columns, (x + 1) * columns) for x in range(X)]
    copies = [fetch(error_ref.at[:, spans[x]], error_buf.at[:, spans[x]], sems.at[x]) for x in range(X)]
    small.wait()
    both = jnp.concatenate(split(q_ref[...]), axis=0)
    first = lax.axis_index("core") == 0
    for x in range(X):
        copies[x].wait()
        term = dot(both, error_buf[:, spans[x]])
        term = (term[:rank] + term[rank:]).astype(BF)
        for z in range(Z):
            at = (x * Z + z) * rank
            zero = term[:, (2 * z) * LANES:(2 * z + 1) * LANES]
            one = term[:, (2 * z + 1) * LANES:(2 * z + 2) * LANES]
            mine_ref[at:at + rank, :] = jnp.where(first, zero, one)
            send_ref[at:at + rank, :] = jnp.where(first, one, zero)


def stack_kernel(*refs):
    for i, ref in enumerate(refs[:-1]):
        refs[-1][i] = ref[...]


def pack_kernel(left_ref, theirs_ref, mine_ref, out_ref):
    left = left_ref[0].astype(F32)
    for z in range(1, Z):
        left = left + left_ref[z].astype(F32)
    left = left.astype(BF)
    tiles = left.shape[0]
    part = (mine_ref[...].astype(F32) + theirs_ref[...].astype(F32)).astype(BF)
    size = part.shape[0] // X
    for x in range(X):
        out_ref[x, :tiles, :] = left
        out_ref[x, tiles:, :] = part[x * size:(x + 1) * size]


def repack_kernel(terms_ref, left_ref, part_ref):
    total = terms_ref[0].astype(F32)
    for x in range(1, X):
        total = total + terms_ref[x].astype(F32)
    total = total.astype(BF)
    tiles = left_ref.shape[0]
    rank = part_ref.shape[1]
    left_ref[...] = total[:tiles]
    for z in range(Z):
        part_ref[z] = total[tiles + z * rank:tiles + (z + 1) * rank]


def slice_kernel(groups, left_ref, part_ref, cotangent_ref, out_ref):
    rank = out_ref.shape[1]
    total = part_ref[0].astype(F32)
    for z in range(1, Z):
        total = total + part_ref[z].astype(F32)
    for b in range(cotangent_ref.shape[0] // LANES):
        total = total + dot(left_ref[b * rank:(b + 1) * rank, :], cotangent_ref[b * LANES:(b + 1) * LANES, :])
    total = total / groups
    for g in range(groups):
        out_ref[g] = total


def spread_kernel(terms_ref, out_ref):
    total = terms_ref[0]
    for g in range(1, terms_ref.shape[0]):
        total = total + terms_ref[g]
    total = total.astype(BF)
    for i in range(out_ref.shape[0]):
        out_ref[i] = total


def ordered_sum(refs, buf):
    n = len(refs)
    for k, ref in enumerate(refs):
        buf[back("dp", k, n)] = ref[...]
    total = buf[0]
    for g in range(1, n):
        total = total + buf[g]
    return total


def slab(ref, step, wide):
    return jnp.concatenate([ref[:, pl.ds(at, wide)] for hop in range(X) for at in columns_of(step, hop, wide)], axis=1)


def wait_all(copies):
    for copy in copies:
        copy.wait()


def piece_kernel(steps, *refs):
    n = len(steps)
    own, other = refs[:n], refs[n:2 * n]
    hidden_hbm, error_hbm, weight_hbm, gate_hbm, up_hbm, matrix_hbm, d_gate_ref, d_up_ref = refs[2 * n:2 * n + 8]
    own_buf, other_buf, hidden_ref, error_ref, weight_ref, gate_ref, up_ref, matrix_ref, sems = refs[2 * n + 8:]
    wide = own_buf.shape[3]
    width = matrix_ref.shape[1] // n
    both = [fetch(hidden_hbm, hidden_ref, sems.at[0, n]), fetch(error_hbm, error_ref, sems.at[1, n])]
    copies = []
    for i in range(n):
        copies.append([fetch(own[i], own_buf.at[i], sems.at[0, i]), fetch(other[i], other_buf.at[i], sems.at[1, i])])
        if i == 0:
            late = [fetch(weight_hbm, weight_ref, sems.at[2, n])]
    pair = [fetch(gate_hbm, gate_ref, sems.at[0, n + 1]), fetch(up_hbm, up_ref, sems.at[1, n + 1])]
    wait_all(both)
    out = []
    total = None
    for i, step in enumerate(steps):
        wait_all(copies[i])
        block = jnp.concatenate([buf[i, hop] for hop in range(X) for buf in (own_buf, other_buf)], axis=1)
        span = pl.ds(i * width, width)
        matrix_ref[:, span] = slab(error_ref, step, wide).astype(F32) + dot(hidden_ref[...], block)
        out.append(fetch(matrix_ref.at[:, span], matrix_hbm.at[:, span], sems.at[2, i]))
        if i == 0:
            wait_all(late)
        term = lax.dot_general(block, slab(weight_ref, step, wide), NT, preferred_element_type=F32)
        total = term if total is None else total + term
    wait_all(pair)
    total = total.T
    gate = gate_ref[...].astype(F32)
    sigma = jax.nn.sigmoid(gate)
    d_gate_ref[...] = (total * up_ref[...].astype(F32) * sigma * (1.0 + gate * (1.0 - sigma))).astype(BF)
    d_up_ref[...] = (total * (gate * sigma)).astype(BF)
    wait_all(out)


def use_pieces(steps, own, other, hidden, error, weight, gate, upward):
    n = len(steps)
    tokens, wide = own[0].shape[1:]
    rows, columns = error.shape
    return call(
        functools.partial(piece_kernel, steps),
        [((rows, columns), F32), ((rows, tokens), BF), ((rows, tokens), BF)],
        [
            pltpu.VMEM((n, X, tokens, wide), BF),
            pltpu.VMEM((n, X, tokens, wide), BF),
            pltpu.VMEM((rows, tokens), BF),
            pltpu.VMEM((rows, columns), BF),
            pltpu.VMEM((rows, columns), BF),
            pltpu.VMEM((rows, tokens), BF),
            pltpu.VMEM((rows, tokens), BF),
            pltpu.VMEM((rows, columns), F32),
            pltpu.SemaphoreType.DMA((3, n + 2)),
        ],
        [HBM] * (2 * n + 5),
        [HBM, None, None],
        flops=4 * rows * tokens * columns,
        moved=30 << 20,
        vmem=52,
    )(*own, *other, hidden, error, weight, gate, upward)


def load_kernel(source_hbm, out_ref, sems):
    part = source_hbm.shape[1] // X
    spans = [pl.ds(i * part, part) for i in range(X)]
    wait_all([fetch(source_hbm.at[:, span], out_ref.at[:, span], sems.at[i]) for i, span in enumerate(spans)])


def turn_kernel(steps, matrix_ref, mine_ref, theirs_ref, out_ref, gram_ref):
    chips = [chip_of(step, hop) for step in steps for hop in range(X)]
    basis = jnp.concatenate([ref[chip] for chip in chips for ref in (mine_ref, theirs_ref)], axis=1)
    gram_ref[...] = lax.dot_general(basis, basis, NT, preferred_element_type=F32)
    out_ref[...] = lax.dot_general(matrix_ref[...].astype(BF), basis, NT, preferred_element_type=F32).T


def inverse_kernel(gram_ref, out_ref):
    n = gram_ref.shape[0]
    row = lax.broadcasted_iota(jnp.int32, (n, 2 * n), 0)
    col = lax.broadcasted_iota(jnp.int32, (n, 2 * n), 1)
    both = jnp.concatenate([gram_ref[...], jnp.zeros((n, n), F32)], axis=1) + jnp.where(col == row + n, 1.0, 0.0)
    for k in range(n):
        pivot = both[k:k + 1, k:k + 1]
        scaled = both[k:k + 1, :] * lax.rsqrt(pivot)
        column_k = both[:, k:k + 1] * lax.rsqrt(pivot)
        both = jnp.where(row > k, both - column_k * scaled, jnp.where(row == k, scaled, both))
    out_ref[...] = both[:, n:]


def final_kernel(steps, groups, *refs):
    matrix_ref, mine_ref, theirs_ref, inverse_ref = refs[:4]
    out_ref, q_ref, buf, terms_buf, sems = refs[4 + groups:]
    wide = mine_ref.shape[2]
    width = CORES * wide
    span = buf.shape[1] // X
    total = ordered_sum(refs[4:4 + groups], terms_buf)
    inverse = inverse_ref[...]
    next_q = jnp.dot(inverse, total / groups, precision=HIGHEST, preferred_element_type=F32)
    q_ref[...] = next_q
    factor = lax.dot_general(inverse, next_q, TN, precision=HIGHEST, preferred_element_type=F32)
    high, low = split(factor.T)
    factor = jnp.concatenate([high, low], axis=1)
    copies = []
    for hop in range(X):
        for i, step in enumerate(steps):
            at = chip_of(step, hop)
            basis = jnp.concatenate([mine_ref[at], theirs_ref[at]], axis=1)
            basis = jnp.concatenate([basis, basis], axis=0)
            start = (i * X + hop) * width
            result = (matrix_ref[:, start:start + width] - dot(factor, basis)).astype(BF)
            for c, place in enumerate(columns_of(step, hop, wide)):
                buf[:, pl.ds(place, wide)] = result[:, c * wide:(c + 1) * wide]
        part = pl.ds(pl.multiple_of(back("x", hop, X) * span, span), span)
        copies.append(fetch(buf.at[:, part], out_ref.at[:, part], sems.at[hop]))
    wait_all(copies)


def local(gate, upward, cotangent, down_weight, error_buffer, start_q):
    groups = lax.axis_size("dp")
    rank = start_q.shape[1]
    tokens, wide = cotangent.shape
    error = error_buffer[0]
    rows, columns = error.shape
    tiles = tokens // LANES * rank
    tie = lax.optimization_barrier

    blocks = [cotangent] + [shift(cotangent, "x", hop, X) for hop in range(1, X)]
    hidden, left = call(
        left_kernel,
        [((rows, tokens), BF), ((tiles, LANES), BF)],
        [
            pltpu.VMEM((rows, tokens), BF),
            pltpu.VMEM((rows, tokens), BF),
            pltpu.VMEM((rank, rows), F32),
            pltpu.VMEM((rows, tokens), BF),
            pltpu.SemaphoreType.DMA((4,)),
        ],
        [HBM] * 3,
        [HBM, VMEM],
        moved=6 * rows * tokens,
    )(gate.T, upward.T, start_q.T)
    theirs = shift(left, "core", 1, CORES)
    send, mine = call(
        error_kernel,
        [((X * Z * rank, wide), BF), ((X * Z * rank, wide), BF)],
        [pltpu.VMEM((rank, rows), F32), pltpu.VMEM((rows, columns), BF), pltpu.SemaphoreType.DMA((X + 1,))],
        [HBM, HBM],
        flops=4 * rows * rank * columns,
        moved=2 * rows * columns,
    )(start_q.T, error)
    part = shift(send, "core", 1, CORES)
    tied = tie((left, theirs, *blocks[1:]))
    left, theirs, blocks[1:] = tied[0], tied[1], tied[2:]
    stacked, = call(stack_kernel, [((X, tokens, wide), BF)], ins=[None] * X, outs=[None])(*blocks)
    pieces, others = {0: stacked}, {}
    steps = (0, 1, 7, 2, 6, 3, 5, 4)

    def ring(step, payload=None):
        up, down = pieces[step - 1], pieces[(Z - step + 1) % Z]
        pieces[step] = shift(up, "z", 1, Z)
        if step < Z // 2:
            pieces[Z - step] = shift(down, "z", Z - 1, Z)
        return payload

    def swap(*steps):
        for step in steps:
            others[step] = shift(pieces[step], "core", 1, CORES)

    left, = call(chip_kernel, [((Z, tiles, LANES), BF)], ins=[VMEM, VMEM])(left, theirs)
    left = ring(1, left)
    swap(0)
    left = exchange(left, "z")
    terms, = call(pack_kernel, [((X, tiles + Z * rank, wide), BF)], ins=[VMEM] * 3)(left, part, mine)
    terms = ring(2, terms)
    swap(1, 7)
    terms = exchange(terms, "x")
    terms, pieces[2], pieces[6] = tie((terms, pieces[2], pieces[6]))
    left, part = call(repack_kernel, [((tiles, LANES), BF), ((Z, rank, wide), BF)], ins=[VMEM])(terms)
    part = ring(3, part)
    swap(2, 6)
    part = exchange(part, "z")
    part, pieces[3], pieces[5] = tie((part, pieces[3], pieces[5]))
    terms, = call(functools.partial(slice_kernel, groups), [((groups, rank, wide), F32)], ins=[VMEM, VMEM, None])(left, part, cotangent)
    terms = ring(4, terms)
    swap(3, 5)
    terms = exchange(terms, "dp")
    terms, pieces[4] = tie((terms, pieces[4]))
    mine, = call(spread_kernel, [((X * Z, rank, wide), BF)], ins=[VMEM])(terms)
    mine = exchange(mine, ("x", "z"))
    swap(4)
    matrix, d_gate, d_up = use_pieces(
        steps, [pieces[s] for s in steps], [others[s] for s in steps], hidden, error, down_weight, gate.T, upward.T)
    mine, matrix = tie((mine, matrix))
    theirs = shift(mine, "core", 1, CORES)
    matrix, = call(load_kernel, [((rows, columns), F32)], [pltpu.SemaphoreType.DMA((X,))], [HBM])(matrix)

    terms, gram = call(
        functools.partial(turn_kernel, steps),
        [((rank, rows), F32), ((rank, rank), F32)],
        ins=[VMEM] * 3,
        flops=2 * rows * rank * columns,
        moved=4 * rows * columns,
    )(matrix, mine, theirs)
    terms = [terms] + [shift(terms, "dp", k, groups) for k in range(1, groups)]
    inverse, = call(inverse_kernel, [((rank, rank), F32)], ins=[VMEM])(gram)

    new_error, next_q = call(
        functools.partial(final_kernel, steps, groups),
        [((rows, columns), BF), ((rank, rows), F32)],
        [pltpu.VMEM((rows, columns), BF), pltpu.VMEM((groups, rank, rows), F32), pltpu.SemaphoreType.DMA((X,))],
        [VMEM] * (4 + groups),
        [HBM, None],
        flops=4 * rows * rank * columns,
        moved=6 * rows * columns,
    )(matrix, mine, theirs, inverse, *terms)
    return (d_gate.T, d_up.T, new_error[None], next_q.T)


def solution(mesh):
    mesh = Mesh(mesh.devices.reshape(mesh.shape["dp"], X, Z, CORES), ("dp",) + PLANE)
    in_specs = (
        P("dp", PLANE),
        P("dp", PLANE),
        P("dp", PLANE),
        P(PLANE, None),
        P("dp", PLANE, None),
        P(PLANE, None),
    )
    out_specs = (P("dp", PLANE), P("dp", PLANE), P("dp", PLANE, None), P(PLANE, None))
    return jax.shard_map(local, mesh=mesh, in_specs=in_specs, out_specs=out_specs, check_vma=False)
```

```python
import functools

import jax
import jax.numpy as jnp
from jax import lax
from jax.experimental import pallas as pl
from jax.experimental.pallas import tpu as pltpu
from jax.sharding import Mesh, PartitionSpec as P

BF = jnp.bfloat16
F32 = jnp.float32
X, Z, CORES = 4, 8, 2
PLANE = ("x", "z", "core")
LANES = 128
NT = (((1,), (1,)), ((), ()))
TN = (((0,), (0,)), ((), ()))
VMEM = pl.BlockSpec(memory_space=pltpu.VMEM)
HBM = pl.BlockSpec(memory_space=pltpu.HBM)
HIGHEST = lax.Precision.HIGHEST


def dot(a, b):
    return jnp.dot(a, b, preferred_element_type=F32)


def split(a):
    high = a.astype(BF)
    return high, (a - high.astype(F32)).astype(BF)


def shift(a, axis, step, n):
    return lax.ppermute(a, axis, [(i, (i + step) % n) for i in range(n)])


def exchange(a, axis):
    return lax.all_to_all(a, axis, 0, 0)


def call(kernel, out, scratch=(), ins=None, outs=None, flops=0, moved=0, vmem=16):
    outs = outs if outs is not None else [VMEM] * len(out)
    run = pl.pallas_call(
        kernel,
        in_specs=[VMEM if spec is None else spec for spec in ins],
        out_specs=[VMEM if spec is None else spec for spec in outs],
        out_shape=[jax.ShapeDtypeStruct(s, t) if spec is None else spec.memory_space(s, t) for spec, (s, t) in zip(outs, out)],
        scratch_shapes=list(scratch),
        cost_estimate=pl.CostEstimate(flops=flops, bytes_accessed=moved, transcendentals=0),
        compiler_params=pltpu.CompilerParams(vmem_limit_bytes=vmem << 20),
    )

    def placed(a, spec):
        return a if spec is None else pltpu.with_memory_space_constraint(a, spec.memory_space)

    return lambda *args: run(*(placed(a, spec) for a, spec in zip(args, ins)))


def back(axis, step, n):
    return lax.rem(lax.axis_index(axis) + (n - step), n)


def chip_of(step, hop):
    return back("x", hop, X) * Z + back("z", step, Z)


def columns_of(step, hop, wide):
    core = lax.axis_index("core")
    return [pl.multiple_of((chip_of(step, hop) * CORES + c) * wide, wide) for c in (core, 1 - core)]


def fetch(source, target, sem):
    copy = pltpu.make_async_copy(source, target, sem)
    copy.start()
    return copy


def left_kernel(gate_hbm, up_hbm, q_hbm, slice_hbm, hidden_hbm, left_ref, slice_ref, gate_ref, up_ref, q_ref, hidden_ref, sems):
    rank = q_ref.shape[0]
    kept = fetch(slice_hbm, slice_ref, sems.at[4])
    for copy in [fetch(a, b, sems.at[i]) for i, (a, b) in enumerate(((gate_hbm, gate_ref), (up_hbm, up_ref), (q_hbm, q_ref)))]:
        copy.wait()
    gate = gate_ref[...].astype(F32)
    hidden = (gate * jax.nn.sigmoid(gate) * up_ref[...].astype(F32)).astype(BF)
    hidden_ref[...] = hidden
    copy = fetch(hidden_ref, hidden_hbm, sems.at[3])
    left = dot(jnp.concatenate(split(q_ref[...]), axis=0), hidden)
    left = (left[:rank] + left[rank:]).astype(BF)
    for b in range(left.shape[1] // LANES):
        left_ref[b * rank:(b + 1) * rank, :] = left[:, b * LANES:(b + 1) * LANES]
    copy.wait()
    kept.wait()


def chip_kernel(left_ref, theirs_ref, out_ref):
    left = (left_ref[...].astype(F32) + theirs_ref[...].astype(F32)).astype(BF)
    for z in range(Z):
        out_ref[z] = left


def error_kernel(q_hbm, error_ref, send_ref, mine_ref, q_ref, error_buf, sems):
    rank = q_ref.shape[0]
    columns = error_ref.shape[1] // X
    small = fetch(q_hbm, q_ref, sems.at[X])
    spans = [slice(x * columns, (x + 1) * columns) for x in range(X)]
    copies = [fetch(error_ref.at[:, spans[x]], error_buf.at[:, spans[x]], sems.at[x]) for x in range(X)]
    small.wait()
    both = jnp.concatenate(split(q_ref[...]), axis=0)
    first = lax.axis_index("core") == 0
    for x in range(X):
        copies[x].wait()
        term = dot(both, error_buf[:, spans[x]])
        term = (term[:rank] + term[rank:]).astype(BF)
        for z in range(Z):
            at = (x * Z + z) * rank
            zero = term[:, (2 * z) * LANES:(2 * z + 1) * LANES]
            one = term[:, (2 * z + 1) * LANES:(2 * z + 2) * LANES]
            mine_ref[at:at + rank, :] = jnp.where(first, zero, one)
            send_ref[at:at + rank, :] = jnp.where(first, one, zero)


def stack_kernel(*refs):
    for i, ref in enumerate(refs[:-1]):
        refs[-1][i] = ref[...]


def pack_kernel(left_ref, theirs_ref, mine_ref, out_ref):
    left = left_ref[0].astype(F32)
    for z in range(1, Z):
        left = left + left_ref[z].astype(F32)
    left = left.astype(BF)
    tiles = left.shape[0]
    part = (mine_ref[...].astype(F32) + theirs_ref[...].astype(F32)).astype(BF)
    size = part.shape[0] // X
    for x in range(X):
        out_ref[x, :tiles, :] = left
        out_ref[x, tiles:, :] = part[x * size:(x + 1) * size]


def repack_kernel(terms_ref, left_ref, part_ref):
    total = terms_ref[0].astype(F32)
    for x in range(1, X):
        total = total + terms_ref[x].astype(F32)
    total = total.astype(BF)
    tiles = left_ref.shape[0]
    rank = part_ref.shape[1]
    left_ref[...] = total[:tiles]
    for z in range(Z):
        part_ref[z] = total[tiles + z * rank:tiles + (z + 1) * rank]


def slice_kernel(groups, left_ref, part_ref, cotangent_ref, out_ref):
    rank = out_ref.shape[1]
    total = part_ref[0].astype(F32)
    for z in range(1, Z):
        total = total + part_ref[z].astype(F32)
    for b in range(cotangent_ref.shape[0] // LANES):
        total = total + dot(left_ref[b * rank:(b + 1) * rank, :], cotangent_ref[b * LANES:(b + 1) * LANES, :])
    total = total / groups
    for g in range(groups):
        out_ref[g] = total


def spread_kernel(terms_ref, out_ref):
    total = terms_ref[0]
    for g in range(1, terms_ref.shape[0]):
        total = total + terms_ref[g]
    total = total.astype(BF)
    for i in range(out_ref.shape[0]):
        out_ref[i] = total


def ordered_sum(refs, buf):
    n = len(refs)
    for k, ref in enumerate(refs):
        buf[back("dp", k, n)] = ref[...]
    total = buf[0]
    for g in range(1, n):
        total = total + buf[g]
    return total


def slab(ref, step, wide):
    return jnp.concatenate([ref[:, pl.ds(at, wide)] for hop in range(X) for at in columns_of(step, hop, wide)], axis=1)


def wait_all(copies):
    for copy in copies:
        copy.wait()


def piece_kernel(steps, *refs):
    n = len(steps)
    own, other = refs[:n], refs[n:2 * n]
    hidden_hbm, error_hbm, weight_hbm, gate_hbm, up_hbm, matrix_hbm, d_gate_ref, d_up_ref = refs[2 * n:2 * n + 8]
    own_buf, other_buf, hidden_ref, error_ref, weight_ref, gate_ref, up_ref, matrix_ref, sems = refs[2 * n + 8:]
    wide = own_buf.shape[3]
    width = matrix_ref.shape[1] // n
    both = [fetch(hidden_hbm, hidden_ref, sems.at[0, n]), fetch(error_hbm, error_ref, sems.at[1, n])]
    copies = []
    for i in range(n):
        copies.append([fetch(own[i], own_buf.at[i], sems.at[0, i]), fetch(other[i], other_buf.at[i], sems.at[1, i])])
        if i == 0:
            late = [fetch(weight_hbm, weight_ref, sems.at[2, n])]
    pair = [fetch(gate_hbm, gate_ref, sems.at[0, n + 1]), fetch(up_hbm, up_ref, sems.at[1, n + 1])]
    wait_all(both)
    out = []
    total = None
    for i, step in enumerate(steps):
        wait_all(copies[i])
        block = jnp.concatenate([buf[i, hop] for hop in range(X) for buf in (own_buf, other_buf)], axis=1)
        span = pl.ds(i * width, width)
        matrix_ref[:, span] = slab(error_ref, step, wide).astype(F32) + dot(hidden_ref[...], block)
        out.append(fetch(matrix_ref.at[:, span], matrix_hbm.at[:, span], sems.at[2, i]))
        if i == 0:
            wait_all(late)
        term = lax.dot_general(block, slab(weight_ref, step, wide), NT, preferred_element_type=F32)
        total = term if total is None else total + term
    wait_all(pair)
    total = total.T
    gate = gate_ref[...].astype(F32)
    sigma = jax.nn.sigmoid(gate)
    d_gate_ref[...] = (total * up_ref[...].astype(F32) * sigma * (1.0 + gate * (1.0 - sigma))).astype(BF)
    d_up_ref[...] = (total * (gate * sigma)).astype(BF)
    wait_all(out)


def use_pieces(steps, own, other, hidden, error, weight, gate, upward):
    n = len(steps)
    tokens, wide = own[0].shape[1:]
    rows, columns = error.shape
    return call(
        functools.partial(piece_kernel, steps),
        [((rows, columns), F32), ((rows, tokens), BF), ((rows, tokens), BF)],
        [
            pltpu.VMEM((n, X, tokens, wide), BF),
            pltpu.VMEM((n, X, tokens, wide), BF),
            pltpu.VMEM((rows, tokens), BF),
            pltpu.VMEM((rows, columns), BF),
            pltpu.VMEM((rows, columns), BF),
            pltpu.VMEM((rows, tokens), BF),
            pltpu.VMEM((rows, tokens), BF),
            pltpu.VMEM((rows, columns), F32),
            pltpu.SemaphoreType.DMA((3, n + 2)),
        ],
        [HBM] * (2 * n + 5),
        [HBM, None, None],
        flops=4 * rows * tokens * columns,
        moved=30 << 20,
        vmem=52,
    )(*own, *other, hidden, error, weight, gate, upward)


def load_kernel(source_hbm, out_ref, sems):
    part = source_hbm.shape[1] // X
    spans = [pl.ds(i * part, part) for i in range(X)]
    wait_all([fetch(source_hbm.at[:, span], out_ref.at[:, span], sems.at[i]) for i, span in enumerate(spans)])


def turn_kernel(steps, matrix_ref, mine_ref, theirs_ref, out_ref, gram_ref):
    chips = [chip_of(step, hop) for step in steps for hop in range(X)]
    basis = jnp.concatenate([ref[chip] for chip in chips for ref in (mine_ref, theirs_ref)], axis=1)
    gram_ref[...] = lax.dot_general(basis, basis, NT, preferred_element_type=F32)
    out_ref[...] = lax.dot_general(matrix_ref[...].astype(BF), basis, NT, preferred_element_type=F32).T


def inverse_kernel(gram_ref, out_ref):
    n = gram_ref.shape[0]
    row = lax.broadcasted_iota(jnp.int32, (n, 2 * n), 0)
    col = lax.broadcasted_iota(jnp.int32, (n, 2 * n), 1)
    both = jnp.concatenate([gram_ref[...], jnp.zeros((n, n), F32)], axis=1) + jnp.where(col == row + n, 1.0, 0.0)
    for k in range(n):
        pivot = both[k:k + 1, k:k + 1]
        scaled = both[k:k + 1, :] * lax.rsqrt(pivot)
        column_k = both[:, k:k + 1] * lax.rsqrt(pivot)
        both = jnp.where(row > k, both - column_k * scaled, jnp.where(row == k, scaled, both))
    out_ref[...] = both[:, n:]


def final_kernel(steps, groups, *refs):
    matrix_ref, mine_ref, theirs_ref, inverse_ref = refs[:4]
    out_ref, q_ref, buf, terms_buf, sems = refs[4 + groups:]
    wide = mine_ref.shape[2]
    width = CORES * wide
    span = buf.shape[1] // X
    total = ordered_sum(refs[4:4 + groups], terms_buf)
    inverse = inverse_ref[...]
    next_q = jnp.dot(inverse, total / groups, precision=HIGHEST, preferred_element_type=F32)
    q_ref[...] = next_q
    factor = lax.dot_general(inverse, next_q, TN, precision=HIGHEST, preferred_element_type=F32)
    high, low = split(factor.T)
    factor = jnp.concatenate([high, low], axis=1)
    copies = []
    for hop in range(X):
        for i, step in enumerate(steps):
            at = chip_of(step, hop)
            basis = jnp.concatenate([mine_ref[at], theirs_ref[at]], axis=1)
            basis = jnp.concatenate([basis, basis], axis=0)
            start = (i * X + hop) * width
            result = (matrix_ref[:, start:start + width] - dot(factor, basis)).astype(BF)
            for c, place in enumerate(columns_of(step, hop, wide)):
                buf[:, pl.ds(place, wide)] = result[:, c * wide:(c + 1) * wide]
        part = pl.ds(pl.multiple_of(back("x", hop, X) * span, span), span)
        copies.append(fetch(buf.at[:, part], out_ref.at[:, part], sems.at[hop]))
    wait_all(copies)


def local(gate, upward, cotangent, down_weight, error_buffer, start_q):
    groups = lax.axis_size("dp")
    rank = start_q.shape[1]
    tokens, wide = cotangent.shape
    error = error_buffer[0]
    rows, columns = error.shape
    tiles = tokens // LANES * rank
    tie = lax.optimization_barrier

    blocks = [cotangent] + [shift(cotangent, "x", hop, X) for hop in range(1, X)]
    hidden, left, blocks[0] = call(
        left_kernel,
        [((rows, tokens), BF), ((tiles, LANES), BF), ((tokens, wide), BF)],
        [
            pltpu.VMEM((rows, tokens), BF),
            pltpu.VMEM((rows, tokens), BF),
            pltpu.VMEM((rank, rows), F32),
            pltpu.VMEM((rows, tokens), BF),
            pltpu.SemaphoreType.DMA((5,)),
        ],
        [HBM] * 4,
        [HBM, VMEM, VMEM],
        moved=6 * rows * tokens,
    )(gate.T, upward.T, start_q.T, cotangent)
    theirs = shift(left, "core", 1, CORES)
    send, mine = call(
        error_kernel,
        [((X * Z * rank, wide), BF), ((X * Z * rank, wide), BF)],
        [pltpu.VMEM((rank, rows), F32), pltpu.VMEM((rows, columns), BF), pltpu.SemaphoreType.DMA((X + 1,))],
        [HBM, HBM],
        flops=4 * rows * rank * columns,
        moved=2 * rows * columns,
    )(start_q.T, error)
    part = shift(send, "core", 1, CORES)
    left, theirs, *blocks = tie((left, theirs, *blocks))
    stacked, = call(stack_kernel, [((X, tokens, wide), BF)], ins=[None] * X, outs=[None])(*blocks)
    pieces, others = {0: stacked}, {}
    steps = (0, 1, 7, 2, 6, 3, 5, 4)

    def ring(step, payload=None):
        up, down = pieces[step - 1], pieces[(Z - step + 1) % Z]
        pieces[step] = shift(up, "z", 1, Z)
        if step < Z // 2:
            pieces[Z - step] = shift(down, "z", Z - 1, Z)
        return payload

    def swap(*steps):
        for step in steps:
            others[step] = shift(pieces[step], "core", 1, CORES)

    left, = call(chip_kernel, [((Z, tiles, LANES), BF)], ins=[VMEM, VMEM])(left, theirs)
    left = ring(1, left)
    swap(0)
    left = exchange(left, "z")
    terms, = call(pack_kernel, [((X, tiles + Z * rank, wide), BF)], ins=[VMEM] * 3)(left, part, mine)
    terms = ring(2, terms)
    swap(1, 7)
    terms = exchange(terms, "x")
    terms, pieces[2], pieces[6] = tie((terms, pieces[2], pieces[6]))
    left, part = call(repack_kernel, [((tiles, LANES), BF), ((Z, rank, wide), BF)], ins=[VMEM])(terms)
    part = ring(3, part)
    swap(2, 6)
    part = exchange(part, "z")
    part, pieces[3], pieces[5] = tie((part, pieces[3], pieces[5]))
    terms, = call(functools.partial(slice_kernel, groups), [((groups, rank, wide), F32)], ins=[VMEM, VMEM, None])(left, part, cotangent)
    terms = ring(4, terms)
    swap(3, 5)
    terms = exchange(terms, "dp")
    terms, pieces[4] = tie((terms, pieces[4]))
    mine, = call(spread_kernel, [((X * Z, rank, wide), BF)], ins=[VMEM])(terms)
    mine = exchange(mine, ("x", "z"))
    swap(4)
    matrix, d_gate, d_up = use_pieces(
        steps, [pieces[s] for s in steps], [others[s] for s in steps], hidden, error, down_weight, gate.T, upward.T)
    mine, matrix = tie((mine, matrix))
    theirs = shift(mine, "core", 1, CORES)
    matrix, = call(load_kernel, [((rows, columns), F32)], [pltpu.SemaphoreType.DMA((X,))], [HBM])(matrix)

    terms, gram = call(
        functools.partial(turn_kernel, steps),
        [((rank, rows), F32), ((rank, rank), F32)],
        ins=[VMEM] * 3,
        flops=2 * rows * rank * columns,
        moved=4 * rows * columns,
    )(matrix, mine, theirs)
    terms = [terms] + [shift(terms, "dp", k, groups) for k in range(1, groups)]
    inverse, = call(inverse_kernel, [((rank, rank), F32)], ins=[VMEM])(gram)

    new_error, next_q = call(
        functools.partial(final_kernel, steps, groups),
        [((rows, columns), BF), ((rank, rows), F32)],
        [pltpu.VMEM((rows, columns), BF), pltpu.VMEM((groups, rank, rows), F32), pltpu.SemaphoreType.DMA((X,))],
        [VMEM] * (4 + groups),
        [HBM, None],
        flops=4 * rows * rank * columns,
        moved=6 * rows * columns,
    )(matrix, mine, theirs, inverse, *terms)
    return (d_gate.T, d_up.T, new_error[None], next_q.T)


def solution(mesh):
    mesh = Mesh(mesh.devices.reshape(mesh.shape["dp"], X, Z, CORES), ("dp",) + PLANE)
    in_specs = (
        P("dp", PLANE),
        P("dp", PLANE),
        P("dp", PLANE),
        P(PLANE, None),
        P("dp", PLANE, None),
        P(PLANE, None),
    )
    out_specs = (P("dp", PLANE), P("dp", PLANE), P("dp", PLANE, None), P(PLANE, None))
    return jax.shard_map(local, mesh=mesh, in_specs=in_specs, out_specs=out_specs, check_vma=False)
```

```python
import functools

import jax
import jax.numpy as jnp
from jax import lax
from jax.experimental import pallas as pl
from jax.experimental.pallas import tpu as pltpu
from jax.sharding import Mesh, PartitionSpec as P

BF = jnp.bfloat16
F32 = jnp.float32
X, Z, CORES = 4, 8, 2
PLANE = ("x", "z", "core")
LANES = 128
NT = (((1,), (1,)), ((), ()))
TN = (((0,), (0,)), ((), ()))
VMEM = pl.BlockSpec(memory_space=pltpu.VMEM)
HBM = pl.BlockSpec(memory_space=pltpu.HBM)
HIGHEST = lax.Precision.HIGHEST


def dot(a, b):
    return jnp.dot(a, b, preferred_element_type=F32)


def split(a):
    high = a.astype(BF)
    return high, (a - high.astype(F32)).astype(BF)


def shift(a, axis, step, n):
    return lax.ppermute(a, axis, [(i, (i + step) % n) for i in range(n)])


def exchange(a, axis):
    return lax.all_to_all(a, axis, 0, 0)


def call(kernel, out, scratch=(), ins=None, outs=None, flops=0, moved=0, vmem=16):
    outs = outs if outs is not None else [VMEM] * len(out)
    run = pl.pallas_call(
        kernel,
        in_specs=[VMEM if spec is None else spec for spec in ins],
        out_specs=[VMEM if spec is None else spec for spec in outs],
        out_shape=[jax.ShapeDtypeStruct(s, t) if spec is None else spec.memory_space(s, t) for spec, (s, t) in zip(outs, out)],
        scratch_shapes=list(scratch),
        cost_estimate=pl.CostEstimate(flops=flops, bytes_accessed=moved, transcendentals=0),
        compiler_params=pltpu.CompilerParams(vmem_limit_bytes=vmem << 20),
    )

    def placed(a, spec):
        return a if spec is None else pltpu.with_memory_space_constraint(a, spec.memory_space)

    return lambda *args: run(*(placed(a, spec) for a, spec in zip(args, ins)))


def back(axis, step, n):
    return lax.rem(lax.axis_index(axis) + (n - step), n)


def chip_of(step, hop):
    return back("x", hop, X) * Z + back("z", step, Z)


def columns_of(step, hop, wide):
    core = lax.axis_index("core")
    return [pl.multiple_of((chip_of(step, hop) * CORES + c) * wide, wide) for c in (core, 1 - core)]


def fetch(source, target, sem):
    copy = pltpu.make_async_copy(source, target, sem)
    copy.start()
    return copy


def left_kernel(gate_hbm, up_hbm, q_hbm, slice_hbm, hidden_hbm, left_ref, slice_ref, gate_ref, up_ref, q_ref, hidden_ref, sems):
    rank = q_ref.shape[0]
    kept = fetch(slice_hbm, slice_ref, sems.at[4])
    for copy in [fetch(a, b, sems.at[i]) for i, (a, b) in enumerate(((gate_hbm, gate_ref), (up_hbm, up_ref), (q_hbm, q_ref)))]:
        copy.wait()
    gate = gate_ref[...].astype(F32)
    hidden = (gate * jax.nn.sigmoid(gate) * up_ref[...].astype(F32)).astype(BF)
    hidden_ref[...] = hidden
    copy = fetch(hidden_ref, hidden_hbm, sems.at[3])
    left = dot(jnp.concatenate(split(q_ref[...]), axis=0), hidden)
    left = (left[:rank] + left[rank:]).astype(BF)
    for b in range(left.shape[1] // LANES):
        left_ref[b * rank:(b + 1) * rank, :] = left[:, b * LANES:(b + 1) * LANES]
    copy.wait()
    kept.wait()


def chip_kernel(left_ref, theirs_ref, out_ref):
    left = (left_ref[...].astype(F32) + theirs_ref[...].astype(F32)).astype(BF)
    for z in range(Z):
        out_ref[z] = left


def error_kernel(q_hbm, error_ref, send_ref, mine_ref, q_ref, error_buf, sems):
    rank = q_ref.shape[0]
    columns = error_ref.shape[1] // X
    small = fetch(q_hbm, q_ref, sems.at[X])
    spans = [slice(x * columns, (x + 1) * columns) for x in range(X)]
    copies = [fetch(error_ref.at[:, spans[x]], error_buf.at[:, spans[x]], sems.at[x]) for x in range(X)]
    small.wait()
    both = jnp.concatenate(split(q_ref[...]), axis=0)
    first = lax.axis_index("core") == 0
    for x in range(X):
        copies[x].wait()
        term = dot(both, error_buf[:, spans[x]])
        term = (term[:rank] + term[rank:]).astype(BF)
        for z in range(Z):
            at = (x * Z + z) * rank
            zero = term[:, (2 * z) * LANES:(2 * z + 1) * LANES]
            one = term[:, (2 * z + 1) * LANES:(2 * z + 2) * LANES]
            mine_ref[at:at + rank, :] = jnp.where(first, zero, one)
            send_ref[at:at + rank, :] = jnp.where(first, one, zero)


def stack_kernel(*refs):
    for i, ref in enumerate(refs[:-1]):
        refs[-1][i] = ref[...]


def pack_kernel(left_ref, theirs_ref, mine_ref, out_ref):
    left = left_ref[0].astype(F32)
    for z in range(1, Z):
        left = left + left_ref[z].astype(F32)
    left = left.astype(BF)
    tiles = left.shape[0]
    part = (mine_ref[...].astype(F32) + theirs_ref[...].astype(F32)).astype(BF)
    size = part.shape[0] // X
    for x in range(X):
        out_ref[x, :tiles, :] = left
        out_ref[x, tiles:, :] = part[x * size:(x + 1) * size]


def repack_kernel(terms_ref, left_ref, part_ref):
    total = terms_ref[0].astype(F32)
    for x in range(1, X):
        total = total + terms_ref[x].astype(F32)
    total = total.astype(BF)
    tiles = left_ref.shape[0]
    rank = part_ref.shape[1]
    left_ref[...] = total[:tiles]
    for z in range(Z):
        part_ref[z] = total[tiles + z * rank:tiles + (z + 1) * rank]


def slice_kernel(groups, left_ref, part_ref, cotangent_ref, out_ref):
    rank = out_ref.shape[1]
    total = part_ref[0].astype(F32)
    for z in range(1, Z):
        total = total + part_ref[z].astype(F32)
    for b in range(cotangent_ref.shape[0] // LANES):
        total = total + dot(left_ref[b * rank:(b + 1) * rank, :], cotangent_ref[b * LANES:(b + 1) * LANES, :])
    total = total / groups
    for g in range(groups):
        out_ref[g] = total


def spread_kernel(terms_ref, out_ref):
    total = terms_ref[0]
    for g in range(1, terms_ref.shape[0]):
        total = total + terms_ref[g]
    total = total.astype(BF)
    for i in range(out_ref.shape[0]):
        out_ref[i] = total


def ordered_sum(refs, buf):
    n = len(refs)
    for k, ref in enumerate(refs):
        buf[back("dp", k, n)] = ref[...]
    total = buf[0]
    for g in range(1, n):
        total = total + buf[g]
    return total


def slab(ref, step, wide):
    return jnp.concatenate([ref[:, pl.ds(at, wide)] for hop in range(X) for at in columns_of(step, hop, wide)], axis=1)


def wait_all(copies):
    for copy in copies:
        copy.wait()


def piece_kernel(steps, *refs):
    n = len(steps)
    own, other = refs[:n], refs[n:2 * n]
    hidden_hbm, error_hbm, weight_hbm, gate_hbm, up_hbm, matrix_hbm, d_gate_ref, d_up_ref = refs[2 * n:2 * n + 8]
    own_buf, other_buf, hidden_ref, error_ref, weight_ref, gate_ref, up_ref, matrix_ref, sems = refs[2 * n + 8:]
    wide = own_buf.shape[3]
    width = matrix_ref.shape[1] // n
    both = [fetch(hidden_hbm, hidden_ref, sems.at[0, n]), fetch(error_hbm, error_ref, sems.at[1, n])]
    copies = []
    for i in range(n):
        copies.append([fetch(own[i], own_buf.at[i], sems.at[0, i]), fetch(other[i], other_buf.at[i], sems.at[1, i])])
        if i == 0:
            late = [fetch(weight_hbm, weight_ref, sems.at[2, n])]
    pair = [fetch(gate_hbm, gate_ref, sems.at[0, n + 1]), fetch(up_hbm, up_ref, sems.at[1, n + 1])]
    wait_all(both)
    out = []
    total = None
    for i, step in enumerate(steps):
        wait_all(copies[i])
        block = jnp.concatenate([buf[i, hop] for hop in range(X) for buf in (own_buf, other_buf)], axis=1)
        span = pl.ds(i * width, width)
        matrix_ref[:, span] = slab(error_ref, step, wide).astype(F32) + dot(hidden_ref[...], block)
        out.append(fetch(matrix_ref.at[:, span], matrix_hbm.at[:, span], sems.at[2, i]))
        if i == 0:
            wait_all(late)
        term = lax.dot_general(block, slab(weight_ref, step, wide), NT, preferred_element_type=F32)
        total = term if total is None else total + term
    wait_all(pair)
    total = total.T
    gate = gate_ref[...].astype(F32)
    sigma = jax.nn.sigmoid(gate)
    d_gate_ref[...] = (total * up_ref[...].astype(F32) * sigma * (1.0 + gate * (1.0 - sigma))).astype(BF)
    d_up_ref[...] = (total * (gate * sigma)).astype(BF)
    wait_all(out)


def use_pieces(steps, own, other, hidden, error, weight, gate, upward):
    n = len(steps)
    tokens, wide = own[0].shape[1:]
    rows, columns = error.shape
    return call(
        functools.partial(piece_kernel, steps),
        [((rows, columns), F32), ((rows, tokens), BF), ((rows, tokens), BF)],
        [
            pltpu.VMEM((n, X, tokens, wide), BF),
            pltpu.VMEM((n, X, tokens, wide), BF),
            pltpu.VMEM((rows, tokens), BF),
            pltpu.VMEM((rows, columns), BF),
            pltpu.VMEM((rows, columns), BF),
            pltpu.VMEM((rows, tokens), BF),
            pltpu.VMEM((rows, tokens), BF),
            pltpu.VMEM((rows, columns), F32),
            pltpu.SemaphoreType.DMA((3, n + 2)),
        ],
        [HBM] * (2 * n + 5),
        [HBM, None, None],
        flops=4 * rows * tokens * columns,
        moved=30 << 20,
        vmem=52,
    )(*own, *other, hidden, error, weight, gate, upward)


def load_kernel(source_hbm, out_ref, sems):
    part = source_hbm.shape[1] // X
    spans = [pl.ds(i * part, part) for i in range(X)]
    wait_all([fetch(source_hbm.at[:, span], out_ref.at[:, span], sems.at[i]) for i, span in enumerate(spans)])


def turn_kernel(steps, matrix_ref, mine_ref, theirs_ref, out_ref, gram_ref):
    chips = [chip_of(step, hop) for step in steps for hop in range(X)]
    basis = jnp.concatenate([ref[chip] for chip in chips for ref in (mine_ref, theirs_ref)], axis=1)
    gram_ref[...] = lax.dot_general(basis, basis, NT, preferred_element_type=F32)
    out_ref[...] = lax.dot_general(matrix_ref[...].astype(BF), basis, NT, preferred_element_type=F32).T


def inverse_kernel(gram_ref, out_ref):
    n = gram_ref.shape[0]
    row = lax.broadcasted_iota(jnp.int32, (n, 2 * n), 0)
    col = lax.broadcasted_iota(jnp.int32, (n, 2 * n), 1)
    both = jnp.concatenate([gram_ref[...], jnp.zeros((n, n), F32)], axis=1) + jnp.where(col == row + n, 1.0, 0.0)
    for k in range(n):
        pivot = both[k:k + 1, k:k + 1]
        scaled = both[k:k + 1, :] * lax.rsqrt(pivot)
        column_k = both[:, k:k + 1] * lax.rsqrt(pivot)
        both = jnp.where(row > k, both - column_k * scaled, jnp.where(row == k, scaled, both))
    out_ref[...] = both[:, n:]


def final_kernel(steps, groups, *refs):
    matrix_ref, mine_ref, theirs_ref, inverse_ref = refs[:4]
    out_ref, q_ref, buf, terms_buf, sems = refs[4 + groups:]
    wide = mine_ref.shape[2]
    width = CORES * wide
    span = buf.shape[1] // X
    total = ordered_sum(refs[4:4 + groups], terms_buf)
    inverse = inverse_ref[...]
    next_q = jnp.dot(inverse, total / groups, precision=HIGHEST, preferred_element_type=F32)
    q_ref[...] = next_q
    factor = lax.dot_general(inverse, next_q, TN, precision=HIGHEST, preferred_element_type=F32)
    high, low = split(factor.T)
    factor = jnp.concatenate([high, low], axis=1)
    copies = []
    for hop in range(X):
        for i, step in enumerate(steps):
            at = chip_of(step, hop)
            basis = jnp.concatenate([mine_ref[at], theirs_ref[at]], axis=1)
            basis = jnp.concatenate([basis, basis], axis=0)
            start = (i * X + hop) * width
            result = (matrix_ref[:, start:start + width] - dot(factor, basis)).astype(BF)
            for c, place in enumerate(columns_of(step, hop, wide)):
                buf[:, pl.ds(place, wide)] = result[:, c * wide:(c + 1) * wide]
        part = pl.ds(pl.multiple_of(back("x", hop, X) * span, span), span)
        copies.append(fetch(buf.at[:, part], out_ref.at[:, part], sems.at[hop]))
    wait_all(copies)


def local(gate, upward, cotangent, down_weight, error_buffer, start_q):
    groups = lax.axis_size("dp")
    rank = start_q.shape[1]
    tokens, wide = cotangent.shape
    error = error_buffer[0]
    rows, columns = error.shape
    tiles = tokens // LANES * rank
    tie = lax.optimization_barrier

    blocks = [cotangent] + [shift(cotangent, "x", hop, X) for hop in range(1, X)]
    hidden, left, blocks[0] = call(
        left_kernel,
        [((rows, tokens), BF), ((tiles, LANES), BF), ((tokens, wide), BF)],
        [
            pltpu.VMEM((rows, tokens), BF),
            pltpu.VMEM((rows, tokens), BF),
            pltpu.VMEM((rank, rows), F32),
            pltpu.VMEM((rows, tokens), BF),
            pltpu.SemaphoreType.DMA((5,)),
        ],
        [HBM] * 4,
        [HBM, VMEM, VMEM],
        moved=6 * rows * tokens,
    )(gate.T, upward.T, start_q.T, cotangent)
    theirs = shift(left, "core", 1, CORES)
    send, mine = call(
        error_kernel,
        [((X * Z * rank, wide), BF), ((X * Z * rank, wide), BF)],
        [pltpu.VMEM((rank, rows), F32), pltpu.VMEM((rows, columns), BF), pltpu.SemaphoreType.DMA((X + 1,))],
        [HBM, HBM],
        flops=4 * rows * rank * columns,
        moved=2 * rows * columns,
    )(start_q.T, error)
    part = shift(send, "core", 1, CORES)
    left, theirs, *blocks = tie((left, theirs, *blocks))
    stacked, = call(stack_kernel, [((X, tokens, wide), BF)], ins=[None] * X, outs=[None])(*blocks)
    pieces, others = {0: stacked}, {}
    steps = (0, 1, 7, 2, 6, 3, 5, 4)

    def ring(step, payload=None):
        up, down = pieces[step - 1], pieces[(Z - step + 1) % Z]
        pieces[step] = shift(up, "z", 1, Z)
        if step < Z // 2:
            pieces[Z - step] = shift(down, "z", Z - 1, Z)
        return payload

    def swap(*steps):
        for step in steps:
            others[step] = shift(pieces[step], "core", 1, CORES)

    left, = call(chip_kernel, [((Z, tiles, LANES), BF)], ins=[VMEM, VMEM])(left, theirs)
    left = ring(1, left)
    swap(0)
    left = exchange(left, "z")
    terms, = call(pack_kernel, [((X, tiles + Z * rank, wide), BF)], ins=[VMEM] * 3)(left, part, mine)
    terms = ring(2, terms)
    swap(1, 7)
    terms = exchange(terms, "x")
    terms, pieces[2], pieces[6] = tie((terms, pieces[2], pieces[6]))
    left, part = call(repack_kernel, [((tiles, LANES), BF), ((Z, rank, wide), BF)], ins=[VMEM])(terms)
    part = ring(3, part)
    swap(2, 6)
    part = exchange(part, "z")
    part, pieces[3], pieces[5] = tie((part, pieces[3], pieces[5]))
    terms, = call(functools.partial(slice_kernel, groups), [((groups, rank, wide), F32)], ins=[VMEM, VMEM, None])(left, part, cotangent)
    terms = ring(4, terms)
    swap(3, 5)
    terms = exchange(terms, "dp")
    terms, pieces[4] = tie((terms, pieces[4]))
    mine, = call(spread_kernel, [((X * Z, rank, wide), BF)], ins=[VMEM])(terms)
    mine, pieces[4] = tie((mine, pieces[4]))
    mine = exchange(mine, ("x", "z"))
    swap(4)
    matrix, d_gate, d_up = use_pieces(
        steps, [pieces[s] for s in steps], [others[s] for s in steps], hidden, error, down_weight, gate.T, upward.T)
    mine, matrix = tie((mine, matrix))
    theirs = shift(mine, "core", 1, CORES)
    matrix, = call(load_kernel, [((rows, columns), F32)], [pltpu.SemaphoreType.DMA((X,))], [HBM])(matrix)

    terms, gram = call(
        functools.partial(turn_kernel, steps),
        [((rank, rows), F32), ((rank, rank), F32)],
        ins=[VMEM] * 3,
        flops=2 * rows * rank * columns,
        moved=4 * rows * columns,
    )(matrix, mine, theirs)
    terms = [terms] + [shift(terms, "dp", k, groups) for k in range(1, groups)]
    inverse, = call(inverse_kernel, [((rank, rank), F32)], ins=[VMEM])(gram)

    new_error, next_q = call(
        functools.partial(final_kernel, steps, groups),
        [((rows, columns), BF), ((rank, rows), F32)],
        [pltpu.VMEM((rows, columns), BF), pltpu.VMEM((groups, rank, rows), F32), pltpu.SemaphoreType.DMA((X,))],
        [VMEM] * (4 + groups),
        [HBM, None],
        flops=4 * rows * rank * columns,
        moved=6 * rows * columns,
    )(matrix, mine, theirs, inverse, *terms)
    return (d_gate.T, d_up.T, new_error[None], next_q.T)


def solution(mesh):
    mesh = Mesh(mesh.devices.reshape(mesh.shape["dp"], X, Z, CORES), ("dp",) + PLANE)
    in_specs = (
        P("dp", PLANE),
        P("dp", PLANE),
        P("dp", PLANE),
        P(PLANE, None),
        P("dp", PLANE, None),
        P(PLANE, None),
    )
    out_specs = (P("dp", PLANE), P("dp", PLANE), P("dp", PLANE, None), P(PLANE, None))
    return jax.shard_map(local, mesh=mesh, in_specs=in_specs, out_specs=out_specs, check_vma=False)
```
